256 devices in a mesh: row: 16 (over z, y_lo), col: 16 (over x, y_hi, core).
Axes of the slice: x: 4, y: 4 (y_hi: 2, y_lo: 2; y = y_hi * 2 + y_lo), z: 8, core: 2. Of those that a mesh axis runs over, the one named last changes fastest.
Arguments:
- z_band: bfloat16 [1024, 768, 128], P('row', 'col'), may hold values from -6 to 6
- z_square: bfloat16 [768, 768, 128], P('row', 'col'), may hold values from -6 to 6
- ln_in_gain: float32 [128], replicated, may hold values from 0.1 to 1.9
- w_a_gate: bfloat16 [128, 128], replicated, may hold values from -0.5 to 0.5
- w_a: bfloat16 [128, 128], replicated, may hold values from -0.5 to 0.5
- w_b_gate: bfloat16 [128, 128], replicated, may hold values from -0.5 to 0.5
- w_b: bfloat16 [128, 128], replicated, may hold values from -0.5 to 0.5
- w_g: bfloat16 [128, 128], replicated, may hold values from -0.5 to 0.5
- ln_out_gain: float32 [128], replicated, may hold values from 0.1 to 1.9
- w_out: bfloat16 [128, 128], replicated, may hold values from -0.5 to 0.5
Outputs:
- update: bfloat16 [1024, 768, 128], P('row', 'col')
The draws below stay inside these ranges and needn't reach their ends.
All inputs are finite; a program needn't handle non-finite values.
Results may differ from the reference program's by a relative error of at most 0.022.
Values may be sent and summed in bfloat16 or wider, within the bound.
No kernel may reach another device: no remote copies, remote signals or barrier semaphores. Data moves between devices by JAX's collectives and lax.ppermute only.
A program may use at most 128 MiB of HBM per device.

```python
import jax
import jax.numpy as jnp
from jax import lax

C = 128
H = 128
R = 1024
K = 768


def block_scale(key, dims, cuts, least, top_value):
    level = 1.0
    for position, blocks in cuts:
        steps = jax.random.uniform(jax.random.fold_in(jax.random.fold_in(key, 6), position), (blocks,), jnp.float32, least / len(cuts), top_value / len(cuts))
        level = level * jnp.repeat(jnp.exp(steps), dims[position] // blocks).reshape((-1,) + (1,) * (len(dims) - 1 - position))
    return level


def gaussian(own_key, dims, deviation, reach, split=(), kind=jnp.bfloat16):
    entries = deviation * jax.random.normal(own_key, dims, jnp.float32)
    if split:
        entries = entries * block_scale(own_key, dims, split, -0.22, 0.18)
    return jnp.clip(entries, -reach, reach).astype(kind)


def setup_inputs(seed: int = 0) -> dict:
    key_list = jax.random.split(jax.random.key(seed), 11)
    return {
        "z_band": gaussian(key_list[0], (R, K, C), 1.0, 6.0, ((0, 16), (1, 16))),
        "z_square": gaussian(key_list[1], (K, K, C), 1.0, 6.0, ((0, 16), (1, 16))),
        "ln_in_gain": jnp.clip(1.0 + 0.18 * jax.random.normal(key_list[2], (C,), jnp.float32), 0.1, 1.9),
        "w_a_gate": gaussian(key_list[3], (C, H), C ** -0.5, 0.5),
        "w_a": gaussian(key_list[4], (C, H), C ** -0.5, 0.5),
        "w_b_gate": gaussian(key_list[5], (C, H), C ** -0.5, 0.5),
        "w_b": gaussian(key_list[6], (C, H), C ** -0.5, 0.5),
        "w_g": gaussian(key_list[7], (C, C), C ** -0.5, 0.5),
        "ln_out_gain": jnp.clip(1.0 + 0.18 * jax.random.normal(key_list[8], (H,), jnp.float32), 0.1, 1.9),
        "w_out": gaussian(key_list[9], (H, C), H ** -0.5, 0.5),
    }


def layer_norm(values, gain):
    mean = lax.optimization_barrier(jnp.mean(values, axis=-1, keepdims=True))
    centred = values - mean
    var = lax.optimization_barrier(jnp.mean(centred * centred, axis=-1, keepdims=True))
    return centred * jax.lax.rsqrt(var + 1e-05) * gain

def gated_edges(normed, gate_weight, value_weight):
    gate = jnp.einsum('ijc,ch->ijh', normed.astype(jnp.float32), gate_weight.astype(jnp.float32))
    value = jnp.einsum('ijc,ch->ijh', normed.astype(jnp.float32), value_weight.astype(jnp.float32))
    return (jax.nn.sigmoid(gate) * value).astype(jnp.bfloat16)

def reference(z_band, z_square, ln_in_gain, w_a_gate, w_a, w_b_gate, w_b, w_g, ln_out_gain, w_out):
    band_norm = layer_norm(z_band.astype(jnp.float32), ln_in_gain).astype(jnp.bfloat16)
    square_norm = layer_norm(z_square.astype(jnp.float32), ln_in_gain).astype(jnp.bfloat16)
    left = gated_edges(band_norm, w_a_gate, w_a)
    right = gated_edges(square_norm, w_b_gate, w_b)
    triangle = jnp.einsum('ikh,jkh->ijh', left.astype(jnp.float32), right.astype(jnp.float32))
    normed = layer_norm(triangle, ln_out_gain).astype(jnp.bfloat16)
    gate = jax.nn.sigmoid(jnp.einsum('ijc,cd->ijd', band_norm.astype(jnp.float32), w_g.astype(jnp.float32)))
    projected = jnp.einsum('ijh,hc->ijc', normed.astype(jnp.float32), w_out.astype(jnp.float32))
    return (gate * projected).astype(jnp.bfloat16)
```

```python
import functools

import jax
import jax.numpy as jnp
from jax import lax
from jax.experimental import pallas as pl
from jax.experimental.pallas import tpu as pltpu
from jax.sharding import Mesh, PartitionSpec as P

F32 = jnp.float32
BF16 = jnp.bfloat16
PARTS = (("z", 8), ("y_lo", 2), ("x", 4), ("y_hi", 2), ("core", 2))
CHIPS = ("z", "y_lo", "x", "y_hi")
ROWS = 16
COLS = 8
LANES = 128
VMEM = 40 * 1024 * 1024


def params():
    return pltpu.CompilerParams(vmem_limit_bytes=VMEM)


def layer_norm(values, gain):
    mean = jnp.mean(values, axis=-1, keepdims=True)
    centred = values - mean
    var = jnp.mean(centred * centred, axis=-1, keepdims=True)
    return centred * lax.rsqrt(var + 1e-05) * gain


def swap(arrays):
    lane = lax.broadcasted_iota(jnp.int32, arrays[0].shape, len(arrays[0].shape) - 1)
    axis = len(arrays[0].shape) - 1
    arrays = list(arrays)
    for bit in range(3):
        shift = 16 << bit
        low = (lane & shift) == 0
        for first in range(8):
            if first & (1 << bit):
                continue
            second = first | (1 << bit)
            a, b = arrays[first], arrays[second]
            arrays[first] = jnp.where(low, a, pltpu.roll(b, shift, axis))
            arrays[second] = jnp.where(low, pltpu.roll(a, LANES - shift, axis), b)
    return arrays


def edges_kernel(band_ref, square_ref, gain_ref, wag_ref, wa_ref, wbg_ref, wb_ref, out_ref, held):
    gain = gain_ref[...]
    for side, (z_ref, gate_ref, value_ref, count) in enumerate(
        ((band_ref, wag_ref, wa_ref, 8), (square_ref, wbg_ref, wb_ref, 6))
    ):
        weights = jnp.concatenate([gate_ref[...].T, value_ref[...].T], axis=0)
        for k3 in range(3):
            for hi in range(count):
                z = z_ref[hi * 8 : hi * 8 + 8, k3 * 16 : k3 * 16 + 16, :].reshape(LANES, LANES)
                normed = layer_norm(z.astype(F32), gain).astype(BF16)
                both = lax.dot_general(
                    weights, normed, (((1,), (1,)), ((), ())), preferred_element_type=F32
                )
                edge = jax.nn.sigmoid(both[:LANES]) * both[LANES:]
                held[pl.ds(side * 24 + k3 * 8 + hi, LANES, stride=48), :] = edge
            if count == 6:
                for hi in (6, 7):
                    held[pl.ds(side * 24 + k3 * 8 + hi, LANES, stride=48), :] = jnp.zeros(
                        (LANES, LANES), F32
                    )
    out_ref[...] = held[...].astype(BF16).reshape(LANES, 48, LANES)


def product_kernel(core_ref, in_ref, own_ref, other_ref, left, right, held):
    def pair(p, carry):
        lefts = []
        for odd in range(2):
            blocks = swap([in_ref[p * 16 + odd * 8 + q].astype(F32) for q in range(8)])
            lefts.append(blocks)
            for lo in range(8):
                held[odd, lo * 24 : lo * 24 + 24, :] = blocks[lo][24:]
        for lo in range(8):
            for k3 in range(3):
                rows = [lefts[odd][lo][k3 * 8 : k3 * 8 + 8] for odd in range(2)]
                left[lo, pl.ds(pl.multiple_of(p * 16, 16), 16), k3 * LANES : k3 * LANES + LANES] = (
                    jnp.concatenate(rows, axis=0).astype(BF16)
                )
        for odd in range(2):
            for k3 in range(3):
                for j3 in range(3):
                    rows = [
                        held[odd, pl.ds(k3 * 8 + j3 * 2 + half, 8, stride=24), :]
                        for half in range(2)
                    ]
                    right[
                        odd,
                        pl.ds(pl.multiple_of(j3 * 128 + p * 16, 16), 16),
                        k3 * LANES : k3 * LANES + LANES,
                    ] = jnp.concatenate(rows, axis=0).astype(BF16)
        return carry

    lax.fori_loop(0, 8, pair, 0)
    core = core_ref[0]
    for lo in range(8):
        for which, ref in ((1 - core, other_ref), (core, own_ref)):
            ref[lo] = lax.dot_general(
                left[lo], right[which], (((1,), (1,)), ((), ())), preferred_element_type=F32
            ).astype(ref.dtype)


def sum_kernel(own_ref, other_ref, out_ref):
    def row(r, carry):
        tiles = []
        both = [
            own_ref[lo, pl.ds(pl.multiple_of(r * 16, 16), 16), :]
            + other_ref[lo, pl.ds(pl.multiple_of(r * 16, 16), 16), :].astype(F32)
            for lo in range(8)
        ]
        for j3 in range(3):
            tiles.append(swap([b[:, j3 * LANES : j3 * LANES + LANES] for b in both]))
        for odd in range(2):
            for q in range(8):
                out_ref[r * 16 + odd * 8 + q] = jnp.concatenate(
                    [tiles[j3][q][odd * 8 : odd * 8 + 8] for j3 in range(3)], axis=0
                ).astype(BF16)
        return carry

    lax.fori_loop(0, 8, row, 0)


def gate_kernel(band_ref, gain_ref, wg_ref, out_ref):
    z = band_ref[...].reshape(-1, LANES)
    normed = layer_norm(z.astype(F32), gain_ref[...]).astype(BF16)
    gate = jax.nn.sigmoid(jnp.dot(normed, wg_ref[...], preferred_element_type=F32))
    out_ref[...] = gate.reshape(out_ref.shape)


def update_kernel(in_ref, gate_ref, gain_ref, wout_ref, out_ref, held):
    held[...] = in_ref[...].astype(F32).reshape(held.shape)
    gain = gain_ref[...]
    for j3 in range(3):
        for hi in range(8):
            tri = held[pl.ds(j3 * 8 + hi, LANES, stride=24), :]
            mean = jnp.mean(tri, axis=0, keepdims=True)
            centred = tri - mean
            var = jnp.mean(centred * centred, axis=0, keepdims=True)
            normed = (centred * lax.rsqrt(var + 1e-05) * gain).astype(BF16)
            projected = lax.dot_general(
                normed, wout_ref[...], (((0,), (0,)), ((), ())), preferred_element_type=F32
            )
            gate = gate_ref[hi * 8 : hi * 8 + 8, j3 * 16 : j3 * 16 + 16, :]
            out_ref[hi * 8 : hi * 8 + 8, j3 * 16 : j3 * 16 + 16, :] = (
                gate * projected.reshape(8, 16, LANES)
            ).astype(BF16)


def shape(dims, kind):
    return jax.ShapeDtypeStruct(dims, kind)


def exchange(values):
    return lax.all_to_all(values, CHIPS, split_axis=0, concat_axis=0, tiled=True)


def shards(z_band, z_square, ln_in_gain, w_a_gate, w_a, w_b_gate, w_b, w_g, ln_out_gain, w_out):
    gain_in = ln_in_gain.reshape(1, LANES)
    gain_out = ln_out_gain.reshape(LANES, 1)
    edges = pl.pallas_call(
        edges_kernel,
        out_shape=shape((LANES, 48, LANES), BF16),
        scratch_shapes=[pltpu.VMEM((LANES * 48, LANES), F32)],
        compiler_params=params(),
        name="edges",
    )(z_band, z_square, gain_in, w_a_gate, w_a, w_b_gate, w_b)
    edges = exchange(edges)
    gate = pl.pallas_call(
        gate_kernel,
        out_shape=shape(z_band.shape, F32),
        compiler_params=params(),
        name="gate",
    )(z_band, gain_in, w_g)
    core = lax.axis_index("core").astype(jnp.int32).reshape(1)
    vmem = pl.BlockSpec(memory_space=pltpu.VMEM)
    own, other = pl.pallas_call(
        product_kernel,
        out_shape=(shape((8, 128, 384), F32), shape((8, 128, 384), BF16)),
        in_specs=[pl.BlockSpec(memory_space=pltpu.SMEM), vmem],
        out_specs=(vmem, vmem),
        scratch_shapes=[
            pltpu.VMEM((8, 128, 384), BF16),
            pltpu.VMEM((2, 384, 384), BF16),
            pltpu.VMEM((2, 8 * 24, LANES), F32),
        ],
        compiler_params=params(),
        name="product",
    )(core, edges)
    other = lax.ppermute(other, "core", ((0, 1), (1, 0)))
    triangle = pl.pallas_call(
        sum_kernel,
        out_shape=shape((LANES, 24, LANES), BF16),
        compiler_params=params(),
        name="sum",
    )(own, other)
    triangle = exchange(triangle)
    return pl.pallas_call(
        update_kernel,
        out_shape=shape(z_band.shape, BF16),
        scratch_shapes=[pltpu.VMEM((LANES * 24, LANES), F32)],
        compiler_params=params(),
        name="update",
    )(triangle, gate, gain_out, w_out)


def solution(mesh):
    names = tuple(name for name, _ in PARTS)
    fine = Mesh(mesh.devices.reshape(tuple(size for _, size in PARTS)), names)
    pair = P(("z", "y_lo"), ("x", "y_hi", "core"), None)
    placed = (pair, pair, P(), P(), P(), P(), P(), P(), P(), P())
    return jax.shard_map(
        shards, mesh=fine, in_specs=placed, out_specs=pair, check_vma=False
    )
```

```python
import functools

import jax
import jax.numpy as jnp
from jax import lax
from jax.experimental import pallas as pl
from jax.experimental.pallas import tpu as pltpu
from jax.sharding import Mesh, PartitionSpec as P

F32 = jnp.float32
BF16 = jnp.bfloat16
PARTS = (("z", 8), ("y_lo", 2), ("x", 4), ("y_hi", 2), ("core", 2))
CHIPS = ("z", "y_lo", "x", "y_hi")
ROWS = 16
COLS = 8
LANES = 128
VMEM = 40 * 1024 * 1024


def params():
    return pltpu.CompilerParams(vmem_limit_bytes=VMEM)


def layer_norm(values, gain):
    mean = jnp.mean(values, axis=-1, keepdims=True)
    centred = values - mean
    var = jnp.mean(centred * centred, axis=-1, keepdims=True)
    return centred * lax.rsqrt(var + 1e-05) * gain


def swap(arrays):
    lane = lax.broadcasted_iota(jnp.int32, arrays[0].shape, len(arrays[0].shape) - 1)
    axis = len(arrays[0].shape) - 1
    arrays = list(arrays)
    for bit in range(3):
        shift = 16 << bit
        low = (lane & shift) == 0
        for first in range(8):
            if first & (1 << bit):
                continue
            second = first | (1 << bit)
            a, b = arrays[first], arrays[second]
            arrays[first] = jnp.where(low, a, pltpu.roll(b, shift, axis))
            arrays[second] = jnp.where(low, pltpu.roll(a, LANES - shift, axis), b)
    return arrays


def edges_kernel(
    band_hbm, square_hbm, gain_hbm, wag_hbm, wa_hbm, wbg_hbm, wb_hbm, out_ref,
    band, square, gain_ref, weights, normed, held, sems,
):
    quarter = band.shape[0] // 4
    parts = [slice(n * quarter, n * quarter + quarter) for n in range(4)]
    pairs = [(gain_hbm, gain_ref)]
    pairs += [(band_hbm.at[part], band.at[part]) for part in parts]
    pairs += [
        (wag_hbm, weights.at[0]),
        (wa_hbm, weights.at[1]),
        (wbg_hbm, weights.at[2]),
        (wb_hbm, weights.at[3]),
        (square_hbm, square),
    ]
    copies = [pltpu.make_async_copy(a, b, sems.at[n]) for n, (a, b) in enumerate(pairs)]
    for copy in copies:
        copy.start()
    share = jnp.full((LANES, LANES), 1.0 / LANES, BF16)
    zeros = jnp.zeros((LANES, LANES), F32)
    for k3 in range(3):
        for hi in (6, 7):
            held[pl.ds(24 + k3 * 8 + hi, LANES, stride=48), :] = zeros
    copies[0].wait()
    gain = gain_ref[...]

    def project(both, rows):
        both = lax.dot_general(both, rows, (((1,), (1,)), ((), ())), preferred_element_type=F32)
        return jax.nn.sigmoid(both[:LANES]) * both[LANES:]

    for part in range(24):
        if part % 6 == 0:
            copies[1 + part // 6].wait()
        rows = slice(part * LANES, part * LANES + LANES)
        z = band[rows, :]
        centred = z.astype(F32) - jnp.dot(z, share, preferred_element_type=F32)
        squares = (centred * centred).astype(BF16)
        var = jnp.dot(squares, share, preferred_element_type=F32)
        normed[rows, :] = centred * lax.rsqrt(var + 1e-05) * gain
    for copy in copies[5:]:
        copy.wait()
    left = jnp.concatenate([weights[0].T, weights[1].T], axis=0)
    right = jnp.concatenate([weights[2].T, weights[3].T], axis=0)
    for step in range(12):
        rows = [
            normed[pl.ds(bit * 24 + step * 2 + odd, 64, stride=48), :]
            for odd in range(2)
            for bit in range(2)
        ]
        edge = project(left, jnp.concatenate(rows, axis=0).astype(BF16))
        for odd in range(2):
            held[pl.ds(step * 2 + odd, LANES, stride=48), :] = edge[:, odd * LANES : odd * LANES + LANES]
        if step < 9:
            k3, hi = step // 3, step % 3 * 2
            z = square[hi * 8 : hi * 8 + 16, k3 * 16 : k3 * 16 + 16, :].reshape(2 * LANES, LANES)
            edge = project(right, layer_norm(z.astype(F32), gain).astype(BF16))
            for odd in range(2):
                held[pl.ds(24 + k3 * 8 + hi + odd, LANES, stride=48), :] = edge[
                    :, odd * LANES : odd * LANES + LANES
                ]
    out_ref[...] = held[...].astype(BF16).reshape(LANES, 48, LANES)


def swap_halves(a, b):
    low = lax.broadcasted_iota(jnp.int32, a.shape, 1) < 64
    moved = pltpu.roll(jnp.where(low, b, a), 64, 1)
    return jnp.where(low, a, moved), jnp.where(low, moved, b)


def product_kernel(core_ref, in_ref, own_ref, other_ref, left, right, held):
    def quad(p, carry):
        base = p * 32
        for half in range(2):
            for q in range(8):
                a, b = swap_halves(
                    *[in_ref[base + half * 16 + odd * 8 + q].astype(F32)[:24] for odd in range(2)]
                )
                blocks = [x[n * 8 : n * 8 + 8] for x in (a, b) for n in range(3)]
                for k3 in range(3):
                    left[p, k3 * LANES + q * 16 : k3 * LANES + q * 16 + 16, half * LANES : half * LANES + LANES] = (
                        jnp.concatenate(blocks[2 * k3 : 2 * k3 + 2], axis=0).astype(BF16)
                    )
        for n in range(4):
            blocks = swap([in_ref[base + n * 8 + q].astype(F32)[24:] for q in range(8)])
            for lo in range(8):
                held[n, lo * 24 : lo * 24 + 24, :] = blocks[lo]
        for core in range(2):
            for k3 in range(3):
                for hi in range(6):
                    rows = [
                        held[half * 2 + core, pl.ds(k3 * 8 + hi, 8, stride=24), :]
                        for half in range(2)
                    ]
                    right[
                        core,
                        pl.ds(pl.multiple_of(hi * 64 + p * 16, 16), 16),
                        k3 * LANES : k3 * LANES + LANES,
                    ] = jnp.concatenate(rows, axis=0).astype(BF16)
        return carry

    lax.fori_loop(0, 4, quad, 0)
    core = core_ref[0]
    for which, ref in ((1 - core, other_ref), (core, own_ref)):
        for p in range(4):
            ref[:, p * 256 : p * 256 + 256] = jnp.dot(
                right[which], left[p], preferred_element_type=F32
            ).astype(ref.dtype)


def sum_kernel(own_ref, other_ref, out_ref):
    for p in range(8):
        lanes = slice(p * LANES, p * LANES + LANES)
        for q2 in range(4):
            tiles = []
            for jh in range(3):
                a, b = [
                    own_ref[start : start + 16, lanes] + other_ref[start : start + 16, lanes].astype(F32)
                    for start in (jh * 64 + q2 * 16, 192 + jh * 64 + q2 * 16)
                ]
                tiles.append(swap_halves(a, b))
            for odd in range(2):
                for n in range(2):
                    out_ref[(p * 2 + odd) * 8 + q2 * 2 + n] = jnp.concatenate(
                        [tiles[jh][odd][n * 8 : n * 8 + 8] for jh in range(3)], axis=0
                    ).astype(BF16)


def gate_kernel(band_ref, gain_ref, wg_ref, out_ref):
    normed = layer_norm(band_ref[...].astype(F32), gain_ref[...]).astype(BF16)
    out_ref[...] = jax.nn.sigmoid(jnp.dot(normed, wg_ref[...], preferred_element_type=F32))


def update_kernel(in_ref, gate_ref, gain_ref, wout_ref, out_ref, held, result):
    held[...] = in_ref[...].astype(F32).reshape(held.shape)
    gain = gain_ref[...]
    for j in range(24):
        tri = held[pl.ds(j, LANES, stride=24), :]
        mean = jnp.mean(tri, axis=0, keepdims=True)
        centred = tri - mean
        var = jnp.mean(centred * centred, axis=0, keepdims=True)
        normed = (centred * lax.rsqrt(var + 1e-05) * gain).astype(BF16)
        projected = lax.dot_general(
            normed, wout_ref[...], (((0,), (0,)), ((), ())), preferred_element_type=F32
        )
        for bit in range(2):
            result[pl.ds(bit * 24 + j, 64, stride=48), :] = projected[bit * 64 : bit * 64 + 64]
    for part in range(24):
        rows = slice(part * LANES, part * LANES + LANES)
        out_ref[rows, :] = (gate_ref[rows, :] * result[rows, :]).astype(BF16)


def shape(dims, kind):
    return jax.ShapeDtypeStruct(dims, kind)


def exchange(values):
    return lax.all_to_all(values, CHIPS, split_axis=0, concat_axis=0, tiled=True)


def shards(z_band, z_square, ln_in_gain, w_a_gate, w_a, w_b_gate, w_b, w_g, ln_out_gain, w_out):
    gain_in = ln_in_gain.reshape(1, LANES)
    gain_out = ln_out_gain.reshape(LANES, 1)
    rows = z_band.shape[0] * z_band.shape[1]
    band = z_band.reshape(rows, LANES)
    vmem = pl.BlockSpec(memory_space=pltpu.VMEM)
    hbm = pl.BlockSpec(memory_space=pltpu.HBM)
    edges = pl.pallas_call(
        edges_kernel,
        out_shape=pltpu.VMEM((LANES, 48, LANES), BF16),
        in_specs=[hbm] * 7,
        out_specs=vmem,
        scratch_shapes=[
            pltpu.VMEM((rows, LANES), BF16),
            pltpu.VMEM(z_square.shape, BF16),
            pltpu.VMEM((1, LANES), F32),
            pltpu.VMEM((4, LANES, LANES), BF16),
            pltpu.VMEM((rows, LANES), F32),
            pltpu.VMEM((LANES * 48, LANES), F32),
            pltpu.SemaphoreType.DMA((10,)),
        ],
        compiler_params=params(),
        name="edges",
    )(*[
        pltpu.with_memory_space_constraint(a, pltpu.HBM)
        for a in (band, z_square, gain_in, w_a_gate, w_a, w_b_gate, w_b)
    ])
    edges = exchange(edges)
    gate = pl.pallas_call(
        gate_kernel,
        out_shape=shape((rows, LANES), F32),
        compiler_params=params(),
        name="gate",
    )(band, gain_in, w_g)
    core = lax.axis_index("core").astype(jnp.int32).reshape(1)
    own, other = pl.pallas_call(
        product_kernel,
        out_shape=(shape((384, 1024), F32), shape((384, 1024), BF16)),
        in_specs=[pl.BlockSpec(memory_space=pltpu.SMEM), vmem],
        out_specs=(vmem, vmem),
        scratch_shapes=[
            pltpu.VMEM((4, 384, 256), BF16),
            pltpu.VMEM((2, 384, 384), BF16),
            pltpu.VMEM((4, 8 * 24, LANES), F32),
        ],
        compiler_params=params(),
        name="product",
    )(core, edges)
    other = lax.ppermute(other, "core", ((0, 1), (1, 0)))
    triangle = pl.pallas_call(
        sum_kernel,
        out_shape=pltpu.VMEM((LANES, 24, LANES), BF16),
        compiler_params=params(),
        name="sum",
    )(own, other)
    triangle = exchange(triangle)
    update = pl.pallas_call(
        update_kernel,
        out_shape=shape((rows, LANES), BF16),
        scratch_shapes=[pltpu.VMEM((LANES * 24, LANES), F32), pltpu.VMEM((rows, LANES), F32)],
        compiler_params=params(),
        name="update",
    )(triangle, gate, gain_out, w_out)
    return update.reshape(z_band.shape)


def solution(mesh):
    names = tuple(name for name, _ in PARTS)
    fine = Mesh(mesh.devices.reshape(tuple(size for _, size in PARTS)), names)
    pair = P(("z", "y_lo"), ("x", "y_hi", "core"), None)
    placed = (pair, pair, P(), P(), P(), P(), P(), P(), P(), P())
    return jax.shard_map(
        shards, mesh=fine, in_specs=placed, out_specs=pair, check_vma=False
    )
```

```python
import functools

import jax
import jax.numpy as jnp
from jax import lax
from jax.experimental import pallas as pl
from jax.experimental.pallas import tpu as pltpu
from jax.sharding import Mesh, PartitionSpec as P

F32 = jnp.float32
BF16 = jnp.bfloat16
PARTS = (("z", 8), ("y_lo", 2), ("x", 4), ("y_hi", 2), ("core", 2))
CHIPS = ("z", "y_lo", "x", "y_hi")
ROWS = 16
COLS = 8
LANES = 128
VMEM = 40 * 1024 * 1024


def params():
    return pltpu.CompilerParams(vmem_limit_bytes=VMEM)


def layer_norm(values, gain):
    mean = jnp.mean(values, axis=-1, keepdims=True)
    centred = values - mean
    var = jnp.mean(centred * centred, axis=-1, keepdims=True)
    return centred * lax.rsqrt(var + 1e-05) * gain


def swap(arrays):
    lane = lax.broadcasted_iota(jnp.int32, arrays[0].shape, len(arrays[0].shape) - 1)
    axis = len(arrays[0].shape) - 1
    arrays = list(arrays)
    for bit in range(3):
        shift = 16 << bit
        low = (lane & shift) == 0
        for first in range(8):
            if first & (1 << bit):
                continue
            second = first | (1 << bit)
            a, b = arrays[first], arrays[second]
            arrays[first] = jnp.where(low, a, pltpu.roll(b, shift, axis))
            arrays[second] = jnp.where(low, pltpu.roll(a, LANES - shift, axis), b)
    return arrays


def edges_kernel(
    band_hbm, square_hbm, gain_hbm, wag_hbm, wa_hbm, wbg_hbm, wb_hbm, out_ref,
    band, square, gain_ref, weights, normed, held, sems,
):
    quarter = band.shape[0] // 4
    parts = [slice(n * quarter, n * quarter + quarter) for n in range(4)]
    pairs = [(gain_hbm, gain_ref)]
    pairs += [(band_hbm.at[part], band.at[part]) for part in parts]
    pairs += [
        (wag_hbm, weights.at[0]),
        (wa_hbm, weights.at[1]),
        (wbg_hbm, weights.at[2]),
        (wb_hbm, weights.at[3]),
        (square_hbm, square),
    ]
    copies = [pltpu.make_async_copy(a, b, sems.at[n]) for n, (a, b) in enumerate(pairs)]
    for copy in copies:
        copy.start()
    share = jnp.full((LANES, LANES), 1.0 / LANES, BF16)
    zeros = jnp.zeros((LANES, LANES), F32)
    for k3 in range(3):
        for hi in (6, 7):
            held[pl.ds(24 + k3 * 8 + hi, LANES, stride=48), :] = zeros
    copies[0].wait()
    gain = gain_ref[...]

    def project(both, rows):
        both = lax.dot_general(both, rows, (((1,), (1,)), ((), ())), preferred_element_type=F32)
        return jax.nn.sigmoid(both[:LANES]) * both[LANES:]

    for part in range(24):
        if part % 6 == 0:
            copies[1 + part // 6].wait()
        rows = slice(part * LANES, part * LANES + LANES)
        z = band[rows, :]
        centred = z.astype(F32) - jnp.dot(z, share, preferred_element_type=F32)
        squares = (centred * centred).astype(BF16)
        var = jnp.dot(squares, share, preferred_element_type=F32)
        normed[rows, :] = centred * lax.rsqrt(var + 1e-05) * gain
    for copy in copies[5:]:
        copy.wait()
    left = jnp.concatenate([weights[0].T, weights[1].T], axis=0)
    right = jnp.concatenate([weights[2].T, weights[3].T], axis=0)
    for step in range(12):
        rows = [
            normed[pl.ds(bit * 24 + step * 2 + odd, 64, stride=48), :]
            for odd in range(2)
            for bit in range(2)
        ]
        edge = project(left, jnp.concatenate(rows, axis=0).astype(BF16))
        for odd in range(2):
            held[pl.ds(step * 2 + odd, LANES, stride=48), :] = edge[:, odd * LANES : odd * LANES + LANES]
        if step < 9:
            k3, hi = step // 3, step % 3 * 2
            z = square[hi * 8 : hi * 8 + 16, k3 * 16 : k3 * 16 + 16, :].reshape(2 * LANES, LANES)
            edge = project(right, layer_norm(z.astype(F32), gain).astype(BF16))
            for odd in range(2):
                held[pl.ds(24 + k3 * 8 + hi + odd, LANES, stride=48), :] = edge[
                    :, odd * LANES : odd * LANES + LANES
                ]
    out_ref[...] = held[...].astype(BF16).reshape(LANES, 48, LANES)


def swap_halves(a, b):
    low = lax.broadcasted_iota(jnp.int32, a.shape, 1) < 64
    moved = pltpu.roll(jnp.where(low, b, a), 64, 1)
    return jnp.where(low, a, moved), jnp.where(low, moved, b)


def product_kernel(core_ref, in_ref, own_ref, other_ref, left, right, held):
    def quad(p, carry):
        base = p * 32
        for half in range(2):
            for q in range(8):
                a, b = swap_halves(
                    *[in_ref[base + half * 16 + odd * 8 + q].astype(F32)[:24] for odd in range(2)]
                )
                blocks = [x[n * 8 : n * 8 + 8] for x in (a, b) for n in range(3)]
                for k3 in range(3):
                    left[p, k3 * LANES + q * 16 : k3 * LANES + q * 16 + 16, half * LANES : half * LANES + LANES] = (
                        jnp.concatenate(blocks[2 * k3 : 2 * k3 + 2], axis=0).astype(BF16)
                    )
        for n in range(4):
            blocks = swap([in_ref[base + n * 8 + q].astype(F32)[24:] for q in range(8)])
            for lo in range(8):
                held[n, lo * 24 : lo * 24 + 24, :] = blocks[lo]
        for core in range(2):
            for k3 in range(3):
                for hi in range(6):
                    rows = [
                        held[half * 2 + core, pl.ds(k3 * 8 + hi, 8, stride=24), :]
                        for half in range(2)
                    ]
                    right[
                        core,
                        pl.ds(pl.multiple_of(hi * 64 + p * 16, 16), 16),
                        k3 * LANES : k3 * LANES + LANES,
                    ] = jnp.concatenate(rows, axis=0).astype(BF16)
        return carry

    lax.fori_loop(0, 4, quad, 0)
    core = core_ref[0]
    for which, ref in ((1 - core, other_ref), (core, own_ref)):
        for p in range(4):
            ref[:, p * 256 : p * 256 + 256] = jnp.dot(
                right[which], left[p], preferred_element_type=F32
            ).astype(ref.dtype)


def sum_kernel(own_ref, other_ref, out_ref):
    for p in range(8):
        lanes = slice(p * LANES, p * LANES + LANES)
        for q2 in range(4):
            tiles = []
            for jh in range(3):
                a, b = [
                    own_ref[start : start + 16, lanes] + other_ref[start : start + 16, lanes].astype(F32)
                    for start in (jh * 64 + q2 * 16, 192 + jh * 64 + q2 * 16)
                ]
                tiles.append(swap_halves(a, b))
            for odd in range(2):
                for n in range(2):
                    out_ref[(p * 2 + odd) * 8 + q2 * 2 + n] = jnp.concatenate(
                        [tiles[jh][odd][n * 8 : n * 8 + 8] for jh in range(3)], axis=0
                    ).astype(BF16)


def gate_kernel(band_ref, gain_ref, wg_ref, out_ref):
    normed = layer_norm(band_ref[...].astype(F32), gain_ref[...]).astype(BF16)
    out_ref[...] = jax.nn.sigmoid(jnp.dot(normed, wg_ref[...], preferred_element_type=F32))


def update_kernel(in_ref, gate_ref, gain_ref, wout_ref, out_ref, held, result):
    held[...] = in_ref[...].astype(F32).reshape(held.shape)
    gain = jnp.broadcast_to(gain_ref[...], (LANES, LANES)).T
    for j in range(24):
        tri = held[pl.ds(j, LANES, stride=24), :]
        mean = jnp.mean(tri, axis=0, keepdims=True)
        centred = tri - mean
        var = jnp.mean(centred * centred, axis=0, keepdims=True)
        normed = (centred * lax.rsqrt(var + 1e-05) * gain).astype(BF16)
        projected = lax.dot_general(
            normed, wout_ref[...], (((0,), (0,)), ((), ())), preferred_element_type=F32
        )
        for bit in range(2):
            result[pl.ds(bit * 24 + j, 64, stride=48), :] = projected[bit * 64 : bit * 64 + 64]
    for part in range(24):
        rows = slice(part * LANES, part * LANES + LANES)
        out_ref[rows, :] = (gate_ref[rows, :] * result[rows, :]).astype(BF16)


def shape(dims, kind):
    return jax.ShapeDtypeStruct(dims, kind)


def exchange(values):
    return lax.all_to_all(values, CHIPS, split_axis=0, concat_axis=0, tiled=True)


def shards(z_band, z_square, ln_in_gain, w_a_gate, w_a, w_b_gate, w_b, w_g, ln_out_gain, w_out):
    gain_in = ln_in_gain.reshape(1, LANES)
    gain_out = ln_out_gain.reshape(1, LANES)
    rows = z_band.shape[0] * z_band.shape[1]
    band = z_band.reshape(rows, LANES)
    vmem = pl.BlockSpec(memory_space=pltpu.VMEM)
    hbm = pl.BlockSpec(memory_space=pltpu.HBM)
    edges = pl.pallas_call(
        edges_kernel,
        out_shape=pltpu.VMEM((LANES, 48, LANES), BF16),
        in_specs=[hbm] * 7,
        out_specs=vmem,
        scratch_shapes=[
            pltpu.VMEM((rows, LANES), BF16),
            pltpu.VMEM(z_square.shape, BF16),
            pltpu.VMEM((1, LANES), F32),
            pltpu.VMEM((4, LANES, LANES), BF16),
            pltpu.VMEM((rows, LANES), F32),
            pltpu.VMEM((LANES * 48, LANES), F32),
            pltpu.SemaphoreType.DMA((10,)),
        ],
        compiler_params=params(),
        name="edges",
    )(*[
        pltpu.with_memory_space_constraint(a, pltpu.HBM)
        for a in (band, z_square, gain_in, w_a_gate, w_a, w_b_gate, w_b)
    ])
    core = lax.axis_index("core").astype(jnp.int32).reshape(1)
    edges, core = lax.optimization_barrier((edges, core))
    edges = exchange(edges)
    own, other = pl.pallas_call(
        product_kernel,
        out_shape=(shape((384, 1024), F32), shape((384, 1024), BF16)),
        in_specs=[pl.BlockSpec(memory_space=pltpu.SMEM), vmem],
        out_specs=(vmem, vmem),
        scratch_shapes=[
            pltpu.VMEM((4, 384, 256), BF16),
            pltpu.VMEM((2, 384, 384), BF16),
            pltpu.VMEM((4, 8 * 24, LANES), F32),
        ],
        compiler_params=params(),
        name="product",
    )(core, edges)
    other, band, gain_in, w_g, gain_out, w_out = lax.optimization_barrier(
        (other, band, gain_in, w_g, gain_out, w_out)
    )
    other = lax.ppermute(other, "core", ((0, 1), (1, 0)))
    gate = pl.pallas_call(
        gate_kernel,
        out_shape=shape((rows, LANES), F32),
        compiler_params=params(),
        name="gate",
    )(band, gain_in, w_g)
    triangle = pl.pallas_call(
        sum_kernel,
        out_shape=pltpu.VMEM((LANES, 24, LANES), BF16),
        compiler_params=params(),
        name="sum",
    )(own, other)
    triangle, gate, gain_out = lax.optimization_barrier((triangle, gate, gain_out))
    triangle = exchange(triangle)
    update = pl.pallas_call(
        update_kernel,
        out_shape=shape((rows, LANES), BF16),
        scratch_shapes=[pltpu.VMEM((LANES * 24, LANES), F32), pltpu.VMEM((rows, LANES), F32)],
        compiler_params=params(),
        name="update",
    )(triangle, gate, gain_out, w_out)
    return update.reshape(z_band.shape)


def solution(mesh):
    names = tuple(name for name, _ in PARTS)
    fine = Mesh(mesh.devices.reshape(tuple(size for _, size in PARTS)), names)
    pair = P(("z", "y_lo"), ("x", "y_hi", "core"), None)
    placed = (pair, pair, P(), P(), P(), P(), P(), P(), P(), P())
    return jax.shard_map(
        shards, mesh=fine, in_specs=placed, out_specs=pair, check_vma=False
    )
```

```python
import functools

import jax
import jax.numpy as jnp
from jax import lax
from jax.experimental import pallas as pl
from jax.experimental.pallas import tpu as pltpu
from jax.sharding import Mesh, PartitionSpec as P

F32 = jnp.float32
BF16 = jnp.bfloat16
PARTS = (("z", 8), ("y_lo", 2), ("x", 4), ("y_hi", 2), ("core", 2))
CHIPS = ("z", "y_lo", "x", "y_hi")
ROWS = 16
COLS = 8
LANES = 128
MESSAGE = 42
VMEM = 40 * 1024 * 1024


def params():
    return pltpu.CompilerParams(vmem_limit_bytes=VMEM)


def layer_norm(values, gain):
    mean = jnp.mean(values, axis=-1, keepdims=True)
    centred = values - mean
    var = jnp.mean(centred * centred, axis=-1, keepdims=True)
    return centred * lax.rsqrt(var + 1e-05) * gain


def swap(arrays):
    lane = lax.broadcasted_iota(jnp.int32, arrays[0].shape, len(arrays[0].shape) - 1)
    axis = len(arrays[0].shape) - 1
    arrays = list(arrays)
    for bit in range(3):
        shift = 16 << bit
        low = (lane & shift) == 0
        for first in range(8):
            if first & (1 << bit):
                continue
            second = first | (1 << bit)
            a, b = arrays[first], arrays[second]
            arrays[first] = jnp.where(low, a, pltpu.roll(b, shift, axis))
            arrays[second] = jnp.where(low, pltpu.roll(a, LANES - shift, axis), b)
    return arrays


def edges_kernel(
    band_hbm, square_hbm, gain_hbm, wag_hbm, wa_hbm, wbg_hbm, wb_hbm, out_ref,
    band, square, gain_ref, weights, normed, held, sems,
):
    quarter = band.shape[0] // 4
    parts = [slice(n * quarter, n * quarter + quarter) for n in range(4)]
    pairs = [(gain_hbm, gain_ref)]
    pairs += [(band_hbm.at[part], band.at[part]) for part in parts]
    pairs += [
        (wag_hbm, weights.at[0]),
        (wa_hbm, weights.at[1]),
        (wbg_hbm, weights.at[2]),
        (wb_hbm, weights.at[3]),
        (square_hbm, square),
    ]
    copies = [pltpu.make_async_copy(a, b, sems.at[n]) for n, (a, b) in enumerate(pairs)]
    for copy in copies:
        copy.start()
    share = jnp.full((LANES, LANES), 1.0 / LANES, BF16)
    copies[0].wait()
    gain = gain_ref[...]

    def project(both, rows):
        both = lax.dot_general(both, rows, (((1,), (1,)), ((), ())), preferred_element_type=F32)
        return jax.nn.sigmoid(both[:LANES]) * both[LANES:]

    for part in range(24):
        if part % 6 == 0:
            copies[1 + part // 6].wait()
        rows = slice(part * LANES, part * LANES + LANES)
        z = band[rows, :]
        centred = z.astype(F32) - jnp.dot(z, share, preferred_element_type=F32)
        squares = (centred * centred).astype(BF16)
        var = jnp.dot(squares, share, preferred_element_type=F32)
        normed[rows, :] = centred * lax.rsqrt(var + 1e-05) * gain
    for copy in copies[5:]:
        copy.wait()
    left = jnp.concatenate([weights[0].T, weights[1].T], axis=0)
    right = jnp.concatenate([weights[2].T, weights[3].T], axis=0)
    for step in range(12):
        rows = [
            normed[pl.ds(bit * 24 + step * 2 + odd, 64, stride=48), :]
            for odd in range(2)
            for bit in range(2)
        ]
        edge = project(left, jnp.concatenate(rows, axis=0).astype(BF16))
        for odd in range(2):
            kb, kk = divmod(step * 2 + odd, 8)
            held[pl.ds(kk * 3 + kb, LANES, stride=MESSAGE), :] = edge[
                :, odd * LANES : odd * LANES + LANES
            ]
        if step < 9:
            k3, hi = step // 3, step % 3 * 2
            z = square[hi * 8 : hi * 8 + 16, k3 * 16 : k3 * 16 + 16, :].reshape(2 * LANES, LANES)
            edge = project(right, layer_norm(z.astype(F32), gain).astype(BF16))
            for odd in range(2):
                held[pl.ds(24 + (hi + odd) * 3 + k3, LANES, stride=MESSAGE), :] = edge[
                    :, odd * LANES : odd * LANES + LANES
                ]
    out_ref[...] = held[...].astype(BF16)


def swap_halves(a, b):
    low = lax.broadcasted_iota(jnp.int32, a.shape, 1) < 64
    moved = pltpu.roll(jnp.where(low, b, a), 64, 1)
    return jnp.where(low, a, moved), jnp.where(low, moved, b)


def product_kernel(core_ref, in_ref, own_ref, other_ref, left, right, raw, held):
    size = 32 * MESSAGE

    def quad(p, carry):
        raw[:size, :] = in_ref[pl.ds(pl.multiple_of(p * size, 16), size), :].astype(F32)

        def rows(n, start):
            return raw[pl.ds(n * MESSAGE + start, 8, stride=3), :]

        for half in range(2):
            for q in range(8):
                n = half * 16 + q
                pairs = [swap_halves(rows(n, kb), rows(n + 8, kb)) for kb in range(3)]
                blocks = [pair[kbit] for kbit in range(2) for pair in pairs]
                for k3 in range(3):
                    left[
                        p,
                        k3 * LANES + q * 16 : k3 * LANES + q * 16 + 16,
                        half * LANES : half * LANES + LANES,
                    ] = jnp.concatenate(blocks[2 * k3 : 2 * k3 + 2], axis=0).astype(BF16)
        for n in range(4):
            for k3 in range(3):
                blocks = swap([rows(n * 8 + q, 24 + k3) for q in range(8)])
                for lo in range(8):
                    held[n, lo * 24 + k3 * 8 : lo * 24 + k3 * 8 + 8, :] = blocks[lo]
        for core in range(2):
            for k3 in range(3):
                for hi in range(6):
                    tiles = [
                        held[half * 2 + core, pl.ds(k3 * 8 + hi, 8, stride=24), :]
                        for half in range(2)
                    ]
                    right[
                        core,
                        pl.ds(pl.multiple_of(hi * 64 + p * 16, 16), 16),
                        k3 * LANES : k3 * LANES + LANES,
                    ] = jnp.concatenate(tiles, axis=0).astype(BF16)
        return carry

    lax.fori_loop(0, 4, quad, 0)
    core = core_ref[0]
    for which, ref in ((1 - core, other_ref), (core, own_ref)):
        for p in range(4):
            ref[:, p * 256 : p * 256 + 256] = jnp.dot(
                right[which], left[p], preferred_element_type=F32
            ).astype(ref.dtype)


def sum_kernel(own_ref, other_ref, out_ref):
    for p in range(8):
        lanes = slice(p * LANES, p * LANES + LANES)
        for q2 in range(4):
            tiles = []
            for jh in range(3):
                a, b = [
                    own_ref[start : start + 16, lanes] + other_ref[start : start + 16, lanes].astype(F32)
                    for start in (jh * 64 + q2 * 16, 192 + jh * 64 + q2 * 16)
                ]
                tiles.append(swap_halves(a, b))
            for odd in range(2):
                for n in range(2):
                    out_ref[(p * 2 + odd) * 8 + q2 * 2 + n] = jnp.concatenate(
                        [tiles[jh][odd][n * 8 : n * 8 + 8] for jh in range(3)], axis=0
                    ).astype(BF16)


def gate_kernel(band_ref, gain_ref, wg_ref, out_ref):
    normed = layer_norm(band_ref[...].astype(F32), gain_ref[...]).astype(BF16)
    out_ref[...] = jax.nn.sigmoid(jnp.dot(normed, wg_ref[...], preferred_element_type=F32))


def update_kernel(in_ref, gate_ref, gain_ref, wout_ref, out_ref, held, result):
    held[...] = in_ref[...].astype(F32).reshape(held.shape)
    gain = jnp.broadcast_to(gain_ref[...], (LANES, LANES)).T
    for j in range(24):
        tri = held[pl.ds(j, LANES, stride=24), :]
        mean = jnp.mean(tri, axis=0, keepdims=True)
        centred = tri - mean
        var = jnp.mean(centred * centred, axis=0, keepdims=True)
        normed = (centred * lax.rsqrt(var + 1e-05) * gain).astype(BF16)
        projected = lax.dot_general(
            normed, wout_ref[...], (((0,), (0,)), ((), ())), preferred_element_type=F32
        )
        for bit in range(2):
            result[pl.ds(bit * 24 + j, 64, stride=48), :] = projected[bit * 64 : bit * 64 + 64]
    for part in range(24):
        rows = slice(part * LANES, part * LANES + LANES)
        out_ref[rows, :] = (gate_ref[rows, :] * result[rows, :]).astype(BF16)


def shape(dims, kind):
    return jax.ShapeDtypeStruct(dims, kind)


def exchange(values):
    return lax.all_to_all(values, CHIPS, split_axis=0, concat_axis=0, tiled=True)


def shards(z_band, z_square, ln_in_gain, w_a_gate, w_a, w_b_gate, w_b, w_g, ln_out_gain, w_out):
    gain_in = ln_in_gain.reshape(1, LANES)
    gain_out = ln_out_gain.reshape(1, LANES)
    rows = z_band.shape[0] * z_band.shape[1]
    band = z_band.reshape(rows, LANES)
    vmem = pl.BlockSpec(memory_space=pltpu.VMEM)
    hbm = pl.BlockSpec(memory_space=pltpu.HBM)
    edges = pl.pallas_call(
        edges_kernel,
        out_shape=pltpu.VMEM((LANES * MESSAGE, LANES), BF16),
        in_specs=[hbm] * 7,
        out_specs=vmem,
        scratch_shapes=[
            pltpu.VMEM((rows, LANES), BF16),
            pltpu.VMEM(z_square.shape, BF16),
            pltpu.VMEM((1, LANES), F32),
            pltpu.VMEM((4, LANES, LANES), BF16),
            pltpu.VMEM((rows, LANES), F32),
            pltpu.VMEM((LANES * MESSAGE, LANES), F32),
            pltpu.SemaphoreType.DMA((10,)),
        ],
        compiler_params=params(),
        name="edges",
    )(*[
        pltpu.with_memory_space_constraint(a, pltpu.HBM)
        for a in (band, z_square, gain_in, w_a_gate, w_a, w_b_gate, w_b)
    ])
    core = lax.axis_index("core").astype(jnp.int32).reshape(1)
    edges, core = lax.optimization_barrier((edges, core))
    edges = exchange(edges.reshape(LANES, MESSAGE // 2, 2, LANES)).reshape(edges.shape)
    own, other = pl.pallas_call(
        product_kernel,
        out_shape=(shape((384, 1024), F32), shape((384, 1024), BF16)),
        in_specs=[pl.BlockSpec(memory_space=pltpu.SMEM), vmem],
        out_specs=(vmem, vmem),
        scratch_shapes=[
            pltpu.VMEM((4, 384, 256), BF16),
            pltpu.VMEM((2, 384, 384), BF16),
            pltpu.VMEM((32 * MESSAGE + 8, LANES), F32),
            pltpu.VMEM((4, 8 * 24, LANES), F32),
        ],
        compiler_params=params(),
        name="product",
    )(core, edges)
    other, band, gain_in, w_g, gain_out, w_out = lax.optimization_barrier(
        (other, band, gain_in, w_g, gain_out, w_out)
    )
    other = lax.ppermute(other, "core", ((0, 1), (1, 0)))
    gate = pl.pallas_call(
        gate_kernel,
        out_shape=shape((rows, LANES), F32),
        compiler_params=params(),
        name="gate",
    )(band, gain_in, w_g)
    triangle = pl.pallas_call(
        sum_kernel,
        out_shape=pltpu.VMEM((LANES, 24, LANES), BF16),
        compiler_params=params(),
        name="sum",
    )(own, other)
    triangle, gate, gain_out = lax.optimization_barrier((triangle, gate, gain_out))
    triangle = exchange(triangle)
    update = pl.pallas_call(
        update_kernel,
        out_shape=shape((rows, LANES), BF16),
        scratch_shapes=[pltpu.VMEM((LANES * 24, LANES), F32), pltpu.VMEM((rows, LANES), F32)],
        compiler_params=params(),
        name="update",
    )(triangle, gate, gain_out, w_out)
    return update.reshape(z_band.shape)


def solution(mesh):
    names = tuple(name for name, _ in PARTS)
    fine = Mesh(mesh.devices.reshape(tuple(size for _, size in PARTS)), names)
    pair = P(("z", "y_lo"), ("x", "y_hi", "core"), None)
    placed = (pair, pair, P(), P(), P(), P(), P(), P(), P(), P())
    return jax.shard_map(
        shards, mesh=fine, in_specs=placed, out_specs=pair, check_vma=False
    )
```

```python
import functools

import jax
import jax.numpy as jnp
from jax import lax
from jax.experimental import pallas as pl
from jax.experimental.pallas import tpu as pltpu
from jax.sharding import Mesh, PartitionSpec as P

F32 = jnp.float32
BF16 = jnp.bfloat16
PARTS = (("z", 8), ("y_lo", 2), ("x", 4), ("y_hi", 2), ("core", 2))
CHIPS = ("z", "y_lo", "x", "y_hi")
ROWS = 16
COLS = 8
LANES = 128
MESSAGE = 42
PITCH = 25
VMEM = 40 * 1024 * 1024


def params():
    return pltpu.CompilerParams(vmem_limit_bytes=VMEM)


def layer_norm(values, gain):
    mean = jnp.mean(values, axis=-1, keepdims=True)
    centred = values - mean
    var = jnp.mean(centred * centred, axis=-1, keepdims=True)
    return centred * lax.rsqrt(var + 1e-05) * gain


def swap(arrays):
    lane = lax.broadcasted_iota(jnp.int32, arrays[0].shape, len(arrays[0].shape) - 1)
    axis = len(arrays[0].shape) - 1
    arrays = list(arrays)
    for bit in range(3):
        shift = 16 << bit
        low = (lane & shift) == 0
        for first in range(8):
            if first & (1 << bit):
                continue
            second = first | (1 << bit)
            a, b = arrays[first], arrays[second]
            if 2 * shift == LANES:
                up = down = pltpu.roll(jnp.where(low, b, a), shift, axis)
            else:
                up, down = pltpu.roll(b, shift, axis), pltpu.roll(a, LANES - shift, axis)
            arrays[first], arrays[second] = jnp.where(low, a, up), jnp.where(low, down, b)
    return arrays


def edges_kernel(
    band_hbm, square_hbm, gain_hbm, wag_hbm, wa_hbm, wbg_hbm, wb_hbm, out_ref,
    band, square, gain_ref, weights, normed, held, sems,
):
    quarter = band.shape[0] // 4
    parts = [slice(n * quarter, n * quarter + quarter) for n in range(4)]
    pairs = [(gain_hbm, gain_ref)]
    pairs += [(band_hbm.at[part], band.at[part]) for part in parts]
    pairs += [
        (wag_hbm, weights.at[0]),
        (wa_hbm, weights.at[1]),
        (wbg_hbm, weights.at[2]),
        (wb_hbm, weights.at[3]),
        (square_hbm, square),
    ]
    copies = [pltpu.make_async_copy(a, b, sems.at[n]) for n, (a, b) in enumerate(pairs)]
    for copy in copies:
        copy.start()
    share = jnp.full((LANES, LANES), 1.0 / LANES, BF16)
    copies[0].wait()
    gain = gain_ref[...]

    def project(both, rows):
        both = lax.dot_general(both, rows, (((1,), (1,)), ((), ())), preferred_element_type=F32)
        return jax.nn.sigmoid(both[:LANES]) * both[LANES:]

    for part in range(24):
        if part % 6 == 0:
            copies[1 + part // 6].wait()
        rows = slice(part * LANES, part * LANES + LANES)
        z = band[rows, :]
        centred = z.astype(F32) - jnp.dot(z, share, preferred_element_type=F32)
        var = jnp.mean(centred * centred, axis=-1, keepdims=True)
        normed[rows, :] = centred * lax.rsqrt(var + 1e-05) * gain
    for copy in copies[5:]:
        copy.wait()
    left = jnp.concatenate([weights[0].T, weights[1].T], axis=0)
    right = jnp.concatenate([weights[2].T, weights[3].T], axis=0)
    for step in range(12):
        rows = [
            normed[pl.ds(bit * 24 + step * 2 + odd, 64, stride=48), :]
            for odd in range(2)
            for bit in range(2)
        ]
        edge = project(left, jnp.concatenate(rows, axis=0).astype(BF16))
        for odd in range(2):
            kb, kk = divmod(step * 2 + odd, 8)
            held[pl.ds(kk * 3 + kb, LANES, stride=MESSAGE), :] = edge[
                :, odd * LANES : odd * LANES + LANES
            ]
        if step < 9:
            k3, hi = step // 3, step % 3 * 2
            z = square[hi * 8 : hi * 8 + 16, k3 * 16 : k3 * 16 + 16, :].reshape(2 * LANES, LANES)
            edge = project(right, layer_norm(z.astype(F32), gain).astype(BF16))
            for odd in range(2):
                held[pl.ds(24 + (hi + odd) * 3 + k3, LANES, stride=MESSAGE), :] = edge[
                    :, odd * LANES : odd * LANES + LANES
                ]
    out_ref[...] = held[...].astype(BF16)


def swap_halves(a, b):
    low = lax.broadcasted_iota(jnp.int32, a.shape, 1) < 64
    moved = pltpu.roll(jnp.where(low, b, a), 64, 1)
    return jnp.where(low, a, moved), jnp.where(low, moved, b)


def product_kernel(core_ref, in_ref, other_ref, left, right, raw, held):
    size = 32 * MESSAGE

    def quad(p, carry):
        raw[:size, :] = in_ref[pl.ds(pl.multiple_of(p * size, 16), size), :].astype(F32)

        def rows(n, start):
            return raw[pl.ds(n * MESSAGE + start, 8, stride=3), :]

        for half in range(2):
            for q in range(8):
                n = half * 16 + q
                pairs = [swap_halves(rows(n, kb), rows(n + 8, kb)) for kb in range(3)]
                blocks = [pair[kbit] for kbit in range(2) for pair in pairs]
                for k3 in range(3):
                    left[
                        p,
                        k3 * LANES + q * 16 : k3 * LANES + q * 16 + 16,
                        half * LANES : half * LANES + LANES,
                    ] = jnp.concatenate(blocks[2 * k3 : 2 * k3 + 2], axis=0).astype(BF16)
        for half in range(2):
            for k3 in range(3):
                blocks = swap([
                    jnp.concatenate(
                        [rows(half * 16 + odd * 8 + q, 24 + k3) for odd in range(2)], axis=0
                    ).astype(BF16)
                    for q in range(8)
                ])
                for lo in range(8):
                    block = blocks[lo].astype(F32)
                    start = lo * PITCH + k3 * 8
                    for odd in range(2):
                        held[half * 2 + odd, start : start + 8, :] = block[odd * 8 : odd * 8 + 8]
        for core in range(2):
            for k3 in range(3):
                for hi in range(6):
                    tiles = [
                        held[half * 2 + core, pl.ds(k3 * 8 + hi, 8, stride=PITCH), :]
                        for half in range(2)
                    ]
                    right[
                        core,
                        pl.ds(pl.multiple_of(hi * 64 + p * 16, 16), 16),
                        k3 * LANES : k3 * LANES + LANES,
                    ] = jnp.concatenate(tiles, axis=0).astype(BF16)
        return carry

    lax.fori_loop(0, 4, quad, 0)
    multiply(right, left, 1 - core_ref[0], other_ref)


def multiply(right, left, core, out_ref):
    for p in range(4):
        out_ref[:, p * 256 : p * 256 + 256] = jnp.dot(
            right[core], left[p], preferred_element_type=F32
        ).astype(out_ref.dtype)


def own_kernel(core_ref, left, right, own_ref):
    multiply(right, left, core_ref[0], own_ref)


def sum_kernel(own_ref, other_ref, out_ref):
    for p in range(8):
        lanes = slice(p * LANES, p * LANES + LANES)
        for q2 in range(4):
            tiles = []
            for jh in range(3):
                a, b = [
                    own_ref[start : start + 16, lanes] + other_ref[start : start + 16, lanes].astype(F32)
                    for start in (jh * 64 + q2 * 16, 192 + jh * 64 + q2 * 16)
                ]
                tiles.append(swap_halves(a, b))
            for odd in range(2):
                for n in range(2):
                    out_ref[(p * 2 + odd) * 8 + q2 * 2 + n] = jnp.concatenate(
                        [tiles[jh][odd][n * 8 : n * 8 + 8] for jh in range(3)], axis=0
                    ).astype(BF16)


def gate_kernel(band_ref, gain_ref, wg_ref, out_ref):
    normed = layer_norm(band_ref[...].astype(F32), gain_ref[...]).astype(BF16)
    out_ref[...] = jax.nn.sigmoid(jnp.dot(normed, wg_ref[...], preferred_element_type=F32))


def update_kernel(in_ref, gate_ref, gain_ref, wout_ref, out_ref, held, result):
    for h in range(LANES):
        held[h * PITCH : h * PITCH + 24, :] = in_ref[h].astype(F32)
    gain = jnp.broadcast_to(gain_ref[...], (LANES, LANES)).T
    for j in range(24):
        tri = held[pl.ds(j, LANES, stride=PITCH), :]
        mean = jnp.mean(tri, axis=0, keepdims=True)
        centred = tri - mean
        var = jnp.mean(centred * centred, axis=0, keepdims=True)
        normed = (centred * lax.rsqrt(var + 1e-05) * gain).astype(BF16)
        projected = lax.dot_general(
            normed, wout_ref[...], (((0,), (0,)), ((), ())), preferred_element_type=F32
        )
        for bit in range(2):
            result[pl.ds(bit * 24 + j, 64, stride=49), :] = projected[bit * 64 : bit * 64 + 64]
    for i in range(64):
        rows = slice(i * 48, i * 48 + 48)
        out_ref[rows, :] = (gate_ref[rows, :] * result[i * 49 : i * 49 + 48, :]).astype(BF16)


def shape(dims, kind):
    return jax.ShapeDtypeStruct(dims, kind)


def exchange(values):
    return lax.all_to_all(values, CHIPS, split_axis=0, concat_axis=0, tiled=True)


def shards(z_band, z_square, ln_in_gain, w_a_gate, w_a, w_b_gate, w_b, w_g, ln_out_gain, w_out):
    gain_in = ln_in_gain.reshape(1, LANES)
    gain_out = ln_out_gain.reshape(1, LANES)
    rows = z_band.shape[0] * z_band.shape[1]
    band = z_band.reshape(rows, LANES)
    vmem = pl.BlockSpec(memory_space=pltpu.VMEM)
    hbm = pl.BlockSpec(memory_space=pltpu.HBM)
    edges = pl.pallas_call(
        edges_kernel,
        out_shape=pltpu.VMEM((LANES * MESSAGE, LANES), BF16),
        in_specs=[hbm] * 7,
        out_specs=vmem,
        scratch_shapes=[
            pltpu.VMEM((rows, LANES), BF16),
            pltpu.VMEM(z_square.shape, BF16),
            pltpu.VMEM((1, LANES), F32),
            pltpu.VMEM((4, LANES, LANES), BF16),
            pltpu.VMEM((rows, LANES), F32),
            pltpu.VMEM((LANES * MESSAGE, LANES), F32),
            pltpu.SemaphoreType.DMA((10,)),
        ],
        compiler_params=params(),
        name="edges",
    )(*[
        pltpu.with_memory_space_constraint(a, pltpu.HBM)
        for a in (band, z_square, gain_in, w_a_gate, w_a, w_b_gate, w_b)
    ])
    core = lax.axis_index("core").astype(jnp.int32).reshape(1)
    edges, core = lax.optimization_barrier((edges, core))
    edges = exchange(edges.reshape(LANES, MESSAGE // 2, 2, LANES)).reshape(edges.shape)
    smem = pl.BlockSpec(memory_space=pltpu.SMEM)
    other, left, right = pl.pallas_call(
        product_kernel,
        out_shape=(
            pltpu.VMEM((384, 1024), BF16),
            pltpu.VMEM((4, 384, 256), BF16),
            pltpu.VMEM((2, 384, 384), BF16),
        ),
        in_specs=[smem, vmem],
        out_specs=(vmem, vmem, vmem),
        scratch_shapes=[
            pltpu.VMEM((32 * MESSAGE + 8, LANES), F32),
            pltpu.VMEM((4, 8 * PITCH + 8, LANES), F32),
        ],
        compiler_params=params(),
        name="product",
    )(core, edges)
    other, band, gain_in, w_g, gain_out, w_out = lax.optimization_barrier(
        (other, band, gain_in, w_g, gain_out, w_out)
    )
    other = lax.ppermute(other, "core", ((0, 1), (1, 0)))
    own = pl.pallas_call(
        own_kernel,
        out_shape=pltpu.VMEM((384, 1024), F32),
        in_specs=[smem, vmem, vmem],
        out_specs=vmem,
        compiler_params=params(),
        name="own",
    )(core, left, right)
    gate = pl.pallas_call(
        gate_kernel,
        out_shape=shape((rows, LANES), F32),
        compiler_params=params(),
        name="gate",
    )(band, gain_in, w_g)
    triangle = pl.pallas_call(
        sum_kernel,
        out_shape=pltpu.VMEM((LANES, 24, LANES), BF16),
        compiler_params=params(),
        name="sum",
    )(own, other)
    triangle, gate, gain_out = lax.optimization_barrier((triangle, gate, gain_out))
    triangle = exchange(triangle)
    update = pl.pallas_call(
        update_kernel,
        out_shape=shape((rows, LANES), BF16),
        scratch_shapes=[pltpu.VMEM((LANES * PITCH, LANES), F32), pltpu.VMEM((64 * 49, LANES), F32)],
        compiler_params=params(),
        name="update",
    )(triangle, gate, gain_out, w_out)
    return update.reshape(z_band.shape)


def solution(mesh):
    names = tuple(name for name, _ in PARTS)
    fine = Mesh(mesh.devices.reshape(tuple(size for _, size in PARTS)), names)
    pair = P(("z", "y_lo"), ("x", "y_hi", "core"), None)
    placed = (pair, pair, P(), P(), P(), P(), P(), P(), P(), P())
    return jax.shard_map(
        shards, mesh=fine, in_specs=placed, out_specs=pair, check_vma=False
    )
```

```python
import functools

import jax
import jax.numpy as jnp
from jax import lax
from jax.experimental import pallas as pl
from jax.experimental.pallas import tpu as pltpu
from jax.sharding import Mesh, PartitionSpec as P

F32 = jnp.float32
BF16 = jnp.bfloat16
PARTS = (("z", 8), ("y_lo", 2), ("x", 4), ("y_hi", 2), ("core", 2))
CHIPS = ("z", "y_lo", "x", "y_hi")
ROWS = 16
COLS = 8
LANES = 128
MESSAGE = 42
PITCH = 25
VMEM = 40 * 1024 * 1024


def params():
    return pltpu.CompilerParams(vmem_limit_bytes=VMEM)


def swap(arrays):
    lane = lax.broadcasted_iota(jnp.int32, arrays[0].shape, len(arrays[0].shape) - 1)
    axis = len(arrays[0].shape) - 1
    arrays = list(arrays)
    for bit in range(3):
        shift = 16 << bit
        low = (lane & shift) == 0
        for first in range(8):
            if first & (1 << bit):
                continue
            second = first | (1 << bit)
            a, b = arrays[first], arrays[second]
            if 2 * shift == LANES:
                up = down = pltpu.roll(jnp.where(low, b, a), shift, axis)
            else:
                up, down = pltpu.roll(b, shift, axis), pltpu.roll(a, LANES - shift, axis)
            arrays[first], arrays[second] = jnp.where(low, a, up), jnp.where(low, down, b)
    return arrays


def edges_kernel(
    band_hbm, square_hbm, gain_hbm, wag_hbm, wa_hbm, wbg_hbm, wb_hbm, out_ref, band_norm,
    band, square, gain_ref, weights, normed, square_norm, held, sems,
):
    quarter = band.shape[0] // 4
    parts = [slice(n * quarter, n * quarter + quarter) for n in range(4)]
    pairs = [(gain_hbm, gain_ref)]
    pairs += [(band_hbm.at[part], band.at[part]) for part in parts]
    pairs += [
        (wag_hbm, weights.at[0]),
        (wa_hbm, weights.at[1]),
        (wbg_hbm, weights.at[2]),
        (wb_hbm, weights.at[3]),
        (square_hbm, square),
    ]
    copies = [pltpu.make_async_copy(a, b, sems.at[n]) for n, (a, b) in enumerate(pairs)]
    for copy in copies:
        copy.start()
    share = jnp.full((LANES, LANES), 1.0 / LANES, BF16)
    copies[0].wait()
    gain = gain_ref[...]

    def project(both, rows):
        both = lax.dot_general(both, rows, (((1,), (1,)), ((), ())), preferred_element_type=F32)
        return jax.nn.sigmoid(both[:LANES]) * both[LANES:]

    def normalise(z):
        centred = z.astype(F32) - jnp.dot(z, share, preferred_element_type=F32)
        var = jnp.mean(centred * centred, axis=-1, keepdims=True)
        return centred * lax.rsqrt(var + 1e-05) * gain

    for part in range(24):
        if part % 6 == 0:
            copies[1 + part // 6].wait()
        rows = slice(part * LANES, part * LANES + LANES)
        norm = normalise(band[rows, :])
        normed[rows, :] = norm
        band_norm[rows, :] = norm.astype(BF16)
    for copy in copies[5:]:
        copy.wait()
    for step in range(9):
        k3, hi = step // 3, step % 3 * 2
        z = square[hi * 8 : hi * 8 + 16, k3 * 16 : k3 * 16 + 16, :].reshape(2 * LANES, LANES)
        square_norm[step] = normalise(z).astype(BF16)
    left = jnp.concatenate([weights[0].T, weights[1].T], axis=0)
    right = jnp.concatenate([weights[2].T, weights[3].T], axis=0)
    for step in range(12):
        rows = [
            normed[pl.ds(bit * 24 + step * 2 + odd, 64, stride=48), :]
            for odd in range(2)
            for bit in range(2)
        ]
        edge = project(left, jnp.concatenate(rows, axis=0).astype(BF16))
        for odd in range(2):
            kb, kk = divmod(step * 2 + odd, 8)
            held[pl.ds(kk * 3 + kb, LANES, stride=MESSAGE), :] = edge[
                :, odd * LANES : odd * LANES + LANES
            ]
        if step < 9:
            k3, hi = step // 3, step % 3 * 2
            edge = project(right, square_norm[step])
            for odd in range(2):
                held[pl.ds(24 + (hi + odd) * 3 + k3, LANES, stride=MESSAGE), :] = edge[
                    :, odd * LANES : odd * LANES + LANES
                ]
    out_ref[...] = held[...].astype(BF16)


def swap_halves(a, b):
    low = lax.broadcasted_iota(jnp.int32, a.shape, 1) < 64
    moved = pltpu.roll(jnp.where(low, b, a), 64, 1)
    return jnp.where(low, a, moved), jnp.where(low, moved, b)


def arrange_right(rows, right, held, p):
    for k3 in range(3):
        blocks = swap([
            jnp.concatenate([rows(half, q, k3) for half in range(2)], axis=0).astype(BF16)
            for q in range(8)
        ])
        for lo in range(8):
            block = blocks[lo].astype(F32)
            start = lo * PITCH + k3 * 8
            for half in range(2):
                held[half, start : start + 8, :] = block[half * 8 : half * 8 + 8]
    for k3 in range(3):
        for hi in range(6):
            tiles = [held[half, pl.ds(k3 * 8 + hi, 8, stride=PITCH), :] for half in range(2)]
            right[
                hi * 64 + p * 16 : hi * 64 + p * 16 + 16, k3 * LANES : k3 * LANES + LANES
            ] = jnp.concatenate(tiles, axis=0).astype(BF16)


def multiply(right, left, out_ref):
    for p in range(4):
        out_ref[:, p * 256 : p * 256 + 256] = jnp.dot(
            right[...], left[p], preferred_element_type=F32
        ).astype(out_ref.dtype)


def product_kernel(core_ref, in_ref, other_ref, left, right, raw, held):
    size = 32 * MESSAGE
    there = pl.multiple_of((1 - core_ref[0]) * (8 * MESSAGE), 8)

    for p in range(4):
        raw[p, :size, :] = in_ref[p * size : p * size + size, :].astype(F32)

        def rows(n, kb, p=p):
            return raw[p, pl.ds(n * MESSAGE + kb, 8, stride=3), :]

        def right_rows(half, q, k3, p=p):
            return raw[p, pl.ds(there + ((half * 16 + q) * MESSAGE + 24 + k3), 8, stride=3), :]

        for half in range(2):
            for q in range(8):
                n = half * 16 + q
                pairs = [swap_halves(rows(n, kb), rows(n + 8, kb)) for kb in range(3)]
                blocks = [pair[kbit] for kbit in range(2) for pair in pairs]
                for k3 in range(3):
                    left[
                        p,
                        k3 * LANES + q * 16 : k3 * LANES + q * 16 + 16,
                        half * LANES : half * LANES + LANES,
                    ] = jnp.concatenate(blocks[2 * k3 : 2 * k3 + 2], axis=0).astype(BF16)
        arrange_right(right_rows, right, held.at[p], p)
    multiply(right, left, other_ref)


def own_kernel(core_ref, in_ref, left, own_ref, right, raw, held):
    size = 8 * MESSAGE
    here = core_ref[0] * size

    for p in range(4):
        for half in range(2):
            start = pl.multiple_of((p * 4 + half * 2) * size + here, 16)
            raw[p, half * size : half * size + size, :] = in_ref[pl.ds(start, size), :].astype(F32)

        def right_rows(half, q, k3, p=p):
            return raw[p, pl.ds((half * 8 + q) * MESSAGE + 24 + k3, 8, stride=3), :]

        arrange_right(right_rows, right, held.at[p], p)
    multiply(right, left, own_ref)


def sum_kernel(own_ref, other_ref, out_ref):
    for p in range(8):
        lanes = slice(p * LANES, p * LANES + LANES)
        for q2 in range(4):
            tiles = []
            for jh in range(3):
                a, b = [
                    own_ref[start : start + 16, lanes] + other_ref[start : start + 16, lanes].astype(F32)
                    for start in (jh * 64 + q2 * 16, 192 + jh * 64 + q2 * 16)
                ]
                tiles.append(swap_halves(a, b))
            for odd in range(2):
                for n in range(2):
                    out_ref[(p * 2 + odd) * 8 + q2 * 2 + n] = jnp.concatenate(
                        [tiles[jh][odd][n * 8 : n * 8 + 8] for jh in range(3)], axis=0
                    ).astype(BF16)


def gate_kernel(norm_ref, wg_ref, out_ref):
    out_ref[...] = jax.nn.sigmoid(
        jnp.dot(norm_ref[...], wg_ref[...], preferred_element_type=F32)
    )


def update_kernel(in_ref, gate_ref, gain_ref, wout_ref, out_ref, held, result):
    for h in range(LANES):
        held[h * PITCH : h * PITCH + 24, :] = in_ref[h].astype(F32)
    gain = jnp.broadcast_to(gain_ref[...], (LANES, LANES)).T
    for j in range(24):
        tri = held[pl.ds(j, LANES, stride=PITCH), :]
        mean = jnp.mean(tri, axis=0, keepdims=True)
        centred = tri - mean
        var = jnp.mean(centred * centred, axis=0, keepdims=True)
        normed = (centred * lax.rsqrt(var + 1e-05) * gain).astype(BF16)
        projected = lax.dot_general(
            normed, wout_ref[...], (((0,), (0,)), ((), ())), preferred_element_type=F32
        )
        for bit in range(2):
            result[pl.ds(bit * 24 + j, 64, stride=49), :] = projected[bit * 64 : bit * 64 + 64]
    for i in range(64):
        rows = slice(i * 48, i * 48 + 48)
        out_ref[rows, :] = (gate_ref[rows, :] * result[i * 49 : i * 49 + 48, :]).astype(BF16)


def shape(dims, kind):
    return jax.ShapeDtypeStruct(dims, kind)


def exchange(values):
    return lax.all_to_all(values, CHIPS, split_axis=0, concat_axis=0, tiled=True)


def shards(z_band, z_square, ln_in_gain, w_a_gate, w_a, w_b_gate, w_b, w_g, ln_out_gain, w_out):
    gain_in = ln_in_gain.reshape(1, LANES)
    gain_out = ln_out_gain.reshape(1, LANES)
    rows = z_band.shape[0] * z_band.shape[1]
    band = z_band.reshape(rows, LANES)
    vmem = pl.BlockSpec(memory_space=pltpu.VMEM)
    hbm = pl.BlockSpec(memory_space=pltpu.HBM)
    edges, band_norm = pl.pallas_call(
        edges_kernel,
        out_shape=(
            pltpu.VMEM((LANES * MESSAGE, LANES), BF16),
            pltpu.VMEM((rows, LANES), BF16),
        ),
        in_specs=[hbm] * 7,
        out_specs=(vmem, vmem),
        scratch_shapes=[
            pltpu.VMEM((rows, LANES), BF16),
            pltpu.VMEM(z_square.shape, BF16),
            pltpu.VMEM((1, LANES), F32),
            pltpu.VMEM((4, LANES, LANES), BF16),
            pltpu.VMEM((rows, LANES), F32),
            pltpu.VMEM((9, 2 * LANES, LANES), BF16),
            pltpu.VMEM((LANES * MESSAGE, LANES), F32),
            pltpu.SemaphoreType.DMA((10,)),
        ],
        compiler_params=params(),
        name="edges",
    )(*[
        pltpu.with_memory_space_constraint(a, pltpu.HBM)
        for a in (band, z_square, gain_in, w_a_gate, w_a, w_b_gate, w_b)
    ])
    core = lax.axis_index("core").astype(jnp.int32).reshape(1)
    edges, core = lax.optimization_barrier((edges, core))
    edges = exchange(edges.reshape(LANES, MESSAGE // 2, 2, LANES)).reshape(edges.shape)
    smem = pl.BlockSpec(memory_space=pltpu.SMEM)
    other, left = pl.pallas_call(
        product_kernel,
        out_shape=(pltpu.VMEM((384, 1024), BF16), pltpu.VMEM((4, 384, 256), BF16)),
        in_specs=[smem, vmem],
        out_specs=(vmem, vmem),
        scratch_shapes=[
            pltpu.VMEM((384, 384), BF16),
            pltpu.VMEM((4, 32 * MESSAGE + 8, LANES), F32),
            pltpu.VMEM((4, 2, 8 * PITCH + 8, LANES), F32),
        ],
        compiler_params=params(),
        name="product",
    )(core, edges)
    other, left, band_norm, gain_out = lax.optimization_barrier((other, left, band_norm, gain_out))
    other = lax.ppermute(other, "core", ((0, 1), (1, 0)))
    own = pl.pallas_call(
        own_kernel,
        out_shape=pltpu.VMEM((384, 1024), F32),
        in_specs=[smem, vmem, vmem],
        out_specs=vmem,
        scratch_shapes=[
            pltpu.VMEM((384, 384), BF16),
            pltpu.VMEM((4, 16 * MESSAGE + 8, LANES), F32),
            pltpu.VMEM((4, 2, 8 * PITCH + 8, LANES), F32),
        ],
        compiler_params=params(),
        name="own",
    )(core, edges, left)
    gate = pl.pallas_call(
        gate_kernel,
        out_shape=shape((rows, LANES), F32),
        compiler_params=params(),
        name="gate",
    )(band_norm, w_g)
    triangle = pl.pallas_call(
        sum_kernel,
        out_shape=pltpu.VMEM((LANES, 24, LANES), BF16),
        compiler_params=params(),
        name="sum",
    )(own, other)
    triangle, gate, gain_out = lax.optimization_barrier((triangle, gate, gain_out))
    triangle = exchange(triangle)
    update = pl.pallas_call(
        update_kernel,
        out_shape=shape((rows, LANES), BF16),
        scratch_shapes=[pltpu.VMEM((LANES * PITCH, LANES), F32), pltpu.VMEM((64 * 49, LANES), F32)],
        compiler_params=params(),
        name="update",
    )(triangle, gate, gain_out, w_out)
    return update.reshape(z_band.shape)


def solution(mesh):
    names = tuple(name for name, _ in PARTS)
    fine = Mesh(mesh.devices.reshape(tuple(size for _, size in PARTS)), names)
    pair = P(("z", "y_lo"), ("x", "y_hi", "core"), None)
    placed = (pair, pair, P(), P(), P(), P(), P(), P(), P(), P())
    return jax.shard_map(
        shards, mesh=fine, in_specs=placed, out_specs=pair, check_vma=False
    )
```

```python
import functools

import jax
import jax.numpy as jnp
from jax import lax
from jax.experimental import pallas as pl
from jax.experimental.pallas import tpu as pltpu
from jax.sharding import Mesh, PartitionSpec as P

F32 = jnp.float32
BF16 = jnp.bfloat16
PARTS = (("z", 8), ("y_lo", 2), ("x", 4), ("y_hi", 2), ("core", 2))
CHIPS = ("z", "y_lo", "x", "y_hi")
ROWS = 16
COLS = 8
LANES = 128
MESSAGE = 42
PITCH = 25
VMEM = 40 * 1024 * 1024


def params():
    return pltpu.CompilerParams(vmem_limit_bytes=VMEM)


def swap(arrays):
    lane = lax.broadcasted_iota(jnp.int32, arrays[0].shape, len(arrays[0].shape) - 1)
    axis = len(arrays[0].shape) - 1
    arrays = list(arrays)
    for bit in range(3):
        shift = 16 << bit
        low = (lane & shift) == 0
        for first in range(8):
            if first & (1 << bit):
                continue
            second = first | (1 << bit)
            a, b = arrays[first], arrays[second]
            if 2 * shift == LANES:
                up = down = pltpu.roll(jnp.where(low, b, a), shift, axis)
            else:
                up, down = pltpu.roll(b, shift, axis), pltpu.roll(a, LANES - shift, axis)
            arrays[first], arrays[second] = jnp.where(low, a, up), jnp.where(low, down, b)
    return arrays


def edges_kernel(
    band_hbm, square_hbm, gain_hbm, wag_hbm, wa_hbm, wbg_hbm, wb_hbm, out_ref, band_norm,
    band, square, gain_ref, weights, normed, square_norm, held, sems,
):
    pairs = [
        (gain_hbm, gain_ref),
        (band_hbm, band),
        (wag_hbm, weights.at[0]),
        (wa_hbm, weights.at[1]),
        (wbg_hbm, weights.at[2]),
        (wb_hbm, weights.at[3]),
        (square_hbm, square),
    ]
    copies = [pltpu.make_async_copy(a, b, sems.at[n]) for n, (a, b) in enumerate(pairs)]
    for copy in copies:
        copy.start()
    share = jnp.full((LANES, LANES), 1.0 / LANES, BF16)
    copies[0].wait()
    gain = gain_ref[...]

    def project(both, rows):
        both = lax.dot_general(both, rows, (((1,), (1,)), ((), ())), preferred_element_type=F32)
        return jax.nn.sigmoid(both[:LANES]) * both[LANES:]

    def normalise(z):
        centred = z.astype(F32) - jnp.dot(z, share, preferred_element_type=F32)
        var = jnp.mean(centred * centred, axis=-1, keepdims=True)
        return centred * lax.rsqrt(var + 1e-05) * gain

    copies[1].wait()
    half = band.shape[0] // 2
    for part in range(2):
        rows = slice(part * half, part * half + half)
        norm = normalise(band[rows, :])
        normed[rows, :] = norm
        band_norm[rows, :] = norm.astype(BF16)
    for copy in copies[2:]:
        copy.wait()
    for step in range(9):
        k3, hi = step // 3, step % 3 * 2
        z = square[hi * 8 : hi * 8 + 16, k3 * 16 : k3 * 16 + 16, :].reshape(2 * LANES, LANES)
        square_norm[step] = normalise(z).astype(BF16)
    left = jnp.concatenate([weights[0].T, weights[1].T], axis=0)
    right = jnp.concatenate([weights[2].T, weights[3].T], axis=0)
    for step in range(12):
        rows = [
            normed[pl.ds(bit * 24 + step * 2 + odd, 64, stride=48), :]
            for odd in range(2)
            for bit in range(2)
        ]
        edge = project(left, jnp.concatenate(rows, axis=0).astype(BF16))
        for odd in range(2):
            kb, kk = divmod(step * 2 + odd, 8)
            held[pl.ds(kk * 3 + kb, LANES, stride=MESSAGE), :] = edge[
                :, odd * LANES : odd * LANES + LANES
            ]
        if step < 9:
            k3, hi = step // 3, step % 3 * 2
            edge = project(right, square_norm[step])
            for odd in range(2):
                held[pl.ds(24 + (hi + odd) * 3 + k3, LANES, stride=MESSAGE), :] = edge[
                    :, odd * LANES : odd * LANES + LANES
                ]
    out_ref[...] = held[...].astype(BF16)


def swap_halves(a, b):
    low = lax.broadcasted_iota(jnp.int32, a.shape, 1) < 64
    moved = pltpu.roll(jnp.where(low, b, a), 64, 1)
    return jnp.where(low, a, moved), jnp.where(low, moved, b)


def arrange_right(rows, right, held, p):
    for k3 in range(3):
        blocks = swap([
            jnp.concatenate([rows(half, q, k3) for half in range(2)], axis=0).astype(BF16)
            for q in range(8)
        ])
        for lo in range(8):
            block = blocks[lo].astype(F32)
            start = lo * PITCH + k3 * 8
            for half in range(2):
                held[half, start : start + 8, :] = block[half * 8 : half * 8 + 8]
    for k3 in range(3):
        for hi in range(6):
            tiles = [held[half, pl.ds(k3 * 8 + hi, 8, stride=PITCH), :] for half in range(2)]
            right[
                hi * 64 + p * 16 : hi * 64 + p * 16 + 16, k3 * LANES : k3 * LANES + LANES
            ] = jnp.concatenate(tiles, axis=0).astype(BF16)


def multiply(right, left, out_ref):
    for p in range(4):
        out_ref[:, p * 256 : p * 256 + 256] = jnp.dot(
            right[...], left[p], preferred_element_type=F32
        ).astype(out_ref.dtype)


def product_kernel(core_ref, in_ref, other_ref, left, right, raw, held):
    size = 32 * MESSAGE
    there = pl.multiple_of((1 - core_ref[0]) * (8 * MESSAGE), 8)

    for p in range(4):
        raw[p, :size, :] = in_ref[p * size : p * size + size, :].astype(F32)

        def rows(n, kb, p=p):
            return raw[p, pl.ds(n * MESSAGE + kb, 8, stride=3), :]

        def right_rows(half, q, k3, p=p):
            return raw[p, pl.ds(there + ((half * 16 + q) * MESSAGE + 24 + k3), 8, stride=3), :]

        for half in range(2):
            for q in range(8):
                n = half * 16 + q
                pairs = [swap_halves(rows(n, kb), rows(n + 8, kb)) for kb in range(3)]
                blocks = [pair[kbit] for kbit in range(2) for pair in pairs]
                for k3 in range(3):
                    left[
                        p,
                        k3 * LANES + q * 16 : k3 * LANES + q * 16 + 16,
                        half * LANES : half * LANES + LANES,
                    ] = jnp.concatenate(blocks[2 * k3 : 2 * k3 + 2], axis=0).astype(BF16)
        arrange_right(right_rows, right, held.at[p], p)
    multiply(right, left, other_ref)


def own_kernel(core_ref, in_ref, left, own_ref, right, raw, held):
    size = 8 * MESSAGE
    here = core_ref[0] * size

    for p in range(4):
        for half in range(2):
            start = pl.multiple_of((p * 4 + half * 2) * size + here, 16)
            raw[p, half * size : half * size + size, :] = in_ref[pl.ds(start, size), :].astype(F32)

        def right_rows(half, q, k3, p=p):
            return raw[p, pl.ds((half * 8 + q) * MESSAGE + 24 + k3, 8, stride=3), :]

        arrange_right(right_rows, right, held.at[p], p)
    multiply(right, left, own_ref)


def sum_kernel(own_ref, other_ref, out_ref):
    for p in range(8):
        lanes = slice(p * LANES, p * LANES + LANES)
        for q2 in range(4):
            tiles = []
            for jh in range(3):
                a, b = [
                    own_ref[start : start + 16, lanes] + other_ref[start : start + 16, lanes].astype(F32)
                    for start in (jh * 64 + q2 * 16, 192 + jh * 64 + q2 * 16)
                ]
                tiles.append(swap_halves(a, b))
            for odd in range(2):
                for n in range(2):
                    out_ref[(p * 2 + odd) * 8 + q2 * 2 + n] = jnp.concatenate(
                        [tiles[jh][odd][n * 8 : n * 8 + 8] for jh in range(3)], axis=0
                    ).astype(BF16)


def gate_kernel(norm_ref, wg_ref, out_ref):
    out_ref[...] = jax.nn.sigmoid(
        jnp.dot(norm_ref[...], wg_ref[...], preferred_element_type=F32)
    )


def update_kernel(in_ref, gate_ref, gain_ref, wout_ref, out_ref, held, result):
    for h in range(LANES):
        held[h * PITCH : h * PITCH + 24, :] = in_ref[h].astype(F32)
    gain = jnp.broadcast_to(gain_ref[...], (LANES, LANES)).T
    for j in range(24):
        tri = held[pl.ds(j, LANES, stride=PITCH), :]
        mean = jnp.mean(tri, axis=0, keepdims=True)
        centred = tri - mean
        var = jnp.mean(centred * centred, axis=0, keepdims=True)
        normed = (centred * lax.rsqrt(var + 1e-05) * gain).astype(BF16)
        projected = lax.dot_general(
            normed, wout_ref[...], (((0,), (0,)), ((), ())), preferred_element_type=F32
        )
        for bit in range(2):
            result[pl.ds(bit * 24 + j, 64, stride=49), :] = projected[bit * 64 : bit * 64 + 64]
    for i in range(64):
        rows = slice(i * 48, i * 48 + 48)
        out_ref[rows, :] = (gate_ref[rows, :] * result[i * 49 : i * 49 + 48, :]).astype(BF16)


def shape(dims, kind):
    return jax.ShapeDtypeStruct(dims, kind)


def exchange(values):
    return lax.all_to_all(values, CHIPS, split_axis=0, concat_axis=0, tiled=True)


def shards(z_band, z_square, ln_in_gain, w_a_gate, w_a, w_b_gate, w_b, w_g, ln_out_gain, w_out):
    gain_in = ln_in_gain.reshape(1, LANES)
    gain_out = ln_out_gain.reshape(1, LANES)
    rows = z_band.shape[0] * z_band.shape[1]
    band = z_band.reshape(rows, LANES)
    vmem = pl.BlockSpec(memory_space=pltpu.VMEM)
    hbm = pl.BlockSpec(memory_space=pltpu.HBM)
    edges, band_norm = pl.pallas_call(
        edges_kernel,
        out_shape=(
            pltpu.VMEM((LANES * MESSAGE, LANES), BF16),
            pltpu.VMEM((rows, LANES), BF16),
        ),
        in_specs=[hbm] * 7,
        out_specs=(vmem, vmem),
        scratch_shapes=[
            pltpu.VMEM((rows, LANES), BF16),
            pltpu.VMEM(z_square.shape, BF16),
            pltpu.VMEM((1, LANES), F32),
            pltpu.VMEM((4, LANES, LANES), BF16),
            pltpu.VMEM((rows, LANES), F32),
            pltpu.VMEM((9, 2 * LANES, LANES), BF16),
            pltpu.VMEM((LANES * MESSAGE, LANES), F32),
            pltpu.SemaphoreType.DMA((7,)),
        ],
        compiler_params=params(),
        name="edges",
    )(*[
        pltpu.with_memory_space_constraint(a, pltpu.HBM)
        for a in (band, z_square, gain_in, w_a_gate, w_a, w_b_gate, w_b)
    ])
    core = lax.axis_index("core").astype(jnp.int32).reshape(1)
    edges, core = lax.optimization_barrier((edges, core))
    edges = exchange(edges.reshape(LANES, MESSAGE // 2, 2, LANES)).reshape(edges.shape)
    smem = pl.BlockSpec(memory_space=pltpu.SMEM)
    other, left = pl.pallas_call(
        product_kernel,
        out_shape=(pltpu.VMEM((384, 1024), BF16), pltpu.VMEM((4, 384, 256), BF16)),
        in_specs=[smem, vmem],
        out_specs=(vmem, vmem),
        scratch_shapes=[
            pltpu.VMEM((384, 384), BF16),
            pltpu.VMEM((4, 32 * MESSAGE + 8, LANES), F32),
            pltpu.VMEM((4, 2, 8 * PITCH + 8, LANES), F32),
        ],
        compiler_params=params(),
        name="product",
    )(core, edges)
    other, left, band_norm, gain_out = lax.optimization_barrier((other, left, band_norm, gain_out))
    other = lax.ppermute(other, "core", ((0, 1), (1, 0)))
    own = pl.pallas_call(
        own_kernel,
        out_shape=pltpu.VMEM((384, 1024), F32),
        in_specs=[smem, vmem, vmem],
        out_specs=vmem,
        scratch_shapes=[
            pltpu.VMEM((384, 384), BF16),
            pltpu.VMEM((4, 16 * MESSAGE + 8, LANES), F32),
            pltpu.VMEM((4, 2, 8 * PITCH + 8, LANES), F32),
        ],
        compiler_params=params(),
        name="own",
    )(core, edges, left)
    gate = pl.pallas_call(
        gate_kernel,
        out_shape=shape((rows, LANES), F32),
        compiler_params=params(),
        name="gate",
    )(band_norm, w_g)
    triangle = pl.pallas_call(
        sum_kernel,
        out_shape=pltpu.VMEM((LANES, 24, LANES), BF16),
        compiler_params=params(),
        name="sum",
    )(own, other)
    triangle, gate, gain_out = lax.optimization_barrier((triangle, gate, gain_out))
    triangle = exchange(triangle)
    update = pl.pallas_call(
        update_kernel,
        out_shape=shape((rows, LANES), BF16),
        scratch_shapes=[pltpu.VMEM((LANES * PITCH, LANES), F32), pltpu.VMEM((64 * 49, LANES), F32)],
        compiler_params=params(),
        name="update",
    )(triangle, gate, gain_out, w_out)
    return update.reshape(z_band.shape)


def solution(mesh):
    names = tuple(name for name, _ in PARTS)
    fine = Mesh(mesh.devices.reshape(tuple(size for _, size in PARTS)), names)
    pair = P(("z", "y_lo"), ("x", "y_hi", "core"), None)
    placed = (pair, pair, P(), P(), P(), P(), P(), P(), P(), P())
    return jax.shard_map(
        shards, mesh=fine, in_specs=placed, out_specs=pair, check_vma=False
    )
```

```python
import functools

import jax
import jax.numpy as jnp
from jax import lax
from jax.experimental import pallas as pl
from jax.experimental.pallas import tpu as pltpu
from jax.sharding import Mesh, PartitionSpec as P

F32 = jnp.float32
BF16 = jnp.bfloat16
PARTS = (("z", 8), ("y_lo", 2), ("x", 4), ("y_hi", 2), ("core", 2))
AXES = tuple(name for name, _ in PARTS)
ROWS = 16
COLS = 8
LANES = 128
MESSAGE = 42
PITCH = 25
VMEM = 40 * 1024 * 1024


def params():
    return pltpu.CompilerParams(vmem_limit_bytes=VMEM)


def swap(arrays):
    lane = lax.broadcasted_iota(jnp.int32, arrays[0].shape, len(arrays[0].shape) - 1)
    axis = len(arrays[0].shape) - 1
    arrays = list(arrays)
    for bit in range(3):
        shift = 16 << bit
        low = (lane & shift) == 0
        for first in range(8):
            if first & (1 << bit):
                continue
            second = first | (1 << bit)
            a, b = arrays[first], arrays[second]
            if 2 * shift == LANES:
                up = down = pltpu.roll(jnp.where(low, b, a), shift, axis)
            else:
                up, down = pltpu.roll(b, shift, axis), pltpu.roll(a, LANES - shift, axis)
            arrays[first], arrays[second] = jnp.where(low, a, up), jnp.where(low, down, b)
    return arrays


def edges_kernel(
    band_hbm, square_hbm, gain_hbm, wag_hbm, wa_hbm, wbg_hbm, wb_hbm, out_ref, band_norm,
    band, square, gain_ref, weights, normed, square_norm, held, sems,
):
    pairs = [
        (gain_hbm, gain_ref),
        (band_hbm, band),
        (wag_hbm, weights.at[0]),
        (wa_hbm, weights.at[1]),
        (wbg_hbm, weights.at[2]),
        (wb_hbm, weights.at[3]),
        (square_hbm, square),
    ]
    copies = [pltpu.make_async_copy(a, b, sems.at[n]) for n, (a, b) in enumerate(pairs)]
    for copy in copies:
        copy.start()
    share = jnp.full((LANES, LANES), 1.0 / LANES, BF16)
    copies[0].wait()
    gain = gain_ref[...]

    def project(both, rows):
        both = lax.dot_general(both, rows, (((1,), (1,)), ((), ())), preferred_element_type=F32)
        return jax.nn.sigmoid(both[:LANES]) * both[LANES:]

    def normalise(z):
        centred = z.astype(F32) - jnp.dot(z, share, preferred_element_type=F32)
        var = jnp.mean(centred * centred, axis=-1, keepdims=True)
        return centred * lax.rsqrt(var + 1e-05) * gain

    copies[1].wait()
    half = band.shape[0] // 2
    for part in range(2):
        rows = slice(part * half, part * half + half)
        norm = normalise(band[rows, :])
        normed[rows, :] = norm
        band_norm[rows, :] = norm.astype(BF16)
    for copy in copies[2:]:
        copy.wait()
    for step in range(9):
        k3, hi = step // 3, step % 3 * 2
        z = square[hi * 8 : hi * 8 + 16, k3 * 16 : k3 * 16 + 16, :].reshape(2 * LANES, LANES)
        square_norm[step] = normalise(z).astype(BF16)
    left = jnp.concatenate([weights[0].T, weights[1].T], axis=0)
    right = jnp.concatenate([weights[2].T, weights[3].T], axis=0)
    for step in range(12):
        rows = [
            normed[pl.ds(bit * 24 + step * 2 + odd, 64, stride=48), :]
            for odd in range(2)
            for bit in range(2)
        ]
        edge = project(left, jnp.concatenate(rows, axis=0).astype(BF16))
        for odd in range(2):
            kb, kk = divmod(step * 2 + odd, 8)
            held[pl.ds(kk * 3 + kb, LANES, stride=MESSAGE), :] = edge[
                :, odd * LANES : odd * LANES + LANES
            ]
        if step < 9:
            k3, hi = step // 3, step % 3 * 2
            edge = project(right, square_norm[step])
            for odd in range(2):
                held[pl.ds(24 + (hi + odd) * 3 + k3, LANES, stride=MESSAGE), :] = edge[
                    :, odd * LANES : odd * LANES + LANES
                ]
    out_ref[...] = held[...].astype(BF16)


def swap_halves(a, b):
    low = lax.broadcasted_iota(jnp.int32, a.shape, 1) < 64
    moved = pltpu.roll(jnp.where(low, b, a), 64, 1)
    return jnp.where(low, a, moved), jnp.where(low, moved, b)


def arrange_right(rows, right, held, p):
    for k3 in range(3):
        blocks = swap([
            jnp.concatenate([rows(half, q, k3) for half in range(2)], axis=0).astype(BF16)
            for q in range(8)
        ])
        for lo in range(8):
            block = blocks[lo].astype(F32)
            start = lo * PITCH + k3 * 8
            for half in range(2):
                held[half, start : start + 8, :] = block[half * 8 : half * 8 + 8]
    for k3 in range(3):
        for hi in range(6):
            tiles = [held[half, pl.ds(k3 * 8 + hi, 8, stride=PITCH), :] for half in range(2)]
            right[
                hi * 64 + p * 16 : hi * 64 + p * 16 + 16, k3 * LANES : k3 * LANES + LANES
            ] = jnp.concatenate(tiles, axis=0).astype(BF16)


def multiply(right, left, out_ref):
    for p in range(4):
        out_ref[:, p * 256 : p * 256 + 256] = jnp.dot(
            right[...], left[p], preferred_element_type=F32
        ).astype(out_ref.dtype)


def product_kernel(core_ref, in_ref, other_ref, left, right, raw, held):
    size = 32 * MESSAGE
    there = pl.multiple_of((1 - core_ref[0]) * (8 * MESSAGE), 8)

    for p in range(4):
        raw[p, :size, :] = in_ref[p * size : p * size + size, :].astype(F32)

        def rows(n, kb, p=p):
            return raw[p, pl.ds(n * MESSAGE + kb, 8, stride=3), :]

        def right_rows(half, q, k3, p=p):
            return raw[p, pl.ds(there + ((half * 16 + q) * MESSAGE + 24 + k3), 8, stride=3), :]

        for half in range(2):
            for q in range(8):
                n = half * 16 + q
                pairs = [swap_halves(rows(n, kb), rows(n + 8, kb)) for kb in range(3)]
                blocks = [pair[kbit] for kbit in range(2) for pair in pairs]
                for k3 in range(3):
                    left[
                        p,
                        k3 * LANES + q * 16 : k3 * LANES + q * 16 + 16,
                        half * LANES : half * LANES + LANES,
                    ] = jnp.concatenate(blocks[2 * k3 : 2 * k3 + 2], axis=0).astype(BF16)
        arrange_right(right_rows, right, held.at[p], p)
    multiply(right, left, other_ref)


def own_kernel(core_ref, in_ref, left, own_ref, right, raw, held):
    size = 8 * MESSAGE
    here = core_ref[0] * size

    for p in range(4):
        for half in range(2):
            start = pl.multiple_of((p * 4 + half * 2) * size + here, 16)
            raw[p, half * size : half * size + size, :] = in_ref[pl.ds(start, size), :].astype(F32)

        def right_rows(half, q, k3, p=p):
            return raw[p, pl.ds((half * 8 + q) * MESSAGE + 24 + k3, 8, stride=3), :]

        arrange_right(right_rows, right, held.at[p], p)
    multiply(right, left, own_ref)


def sum_kernel(own_ref, other_ref, out_ref):
    for p in range(8):
        lanes = slice(p * LANES, p * LANES + LANES)
        for q2 in range(4):
            tiles = []
            for jh in range(3):
                a, b = [
                    own_ref[start : start + 16, lanes] + other_ref[start : start + 16, lanes].astype(F32)
                    for start in (jh * 64 + q2 * 16, 192 + jh * 64 + q2 * 16)
                ]
                tiles.append(swap_halves(a, b))
            for odd in range(2):
                for n in range(2):
                    out_ref[(p * 2 + odd) * 8 + q2 * 2 + n] = jnp.concatenate(
                        [tiles[jh][odd][n * 8 : n * 8 + 8] for jh in range(3)], axis=0
                    ).astype(BF16)


def gate_kernel(norm_ref, wg_ref, out_ref):
    out_ref[...] = jax.nn.sigmoid(
        jnp.dot(norm_ref[...], wg_ref[...], preferred_element_type=F32)
    )


def update_kernel(in_ref, gate_ref, gain_ref, wout_ref, out_ref, held, result):
    for h in range(LANES):
        held[h * PITCH : h * PITCH + 24, :] = in_ref[h].astype(F32)
    gain = jnp.broadcast_to(gain_ref[...], (LANES, LANES)).T
    for j in range(24):
        tri = held[pl.ds(j, LANES, stride=PITCH), :]
        mean = jnp.mean(tri, axis=0, keepdims=True)
        centred = tri - mean
        var = jnp.mean(centred * centred, axis=0, keepdims=True)
        normed = (centred * lax.rsqrt(var + 1e-05) * gain).astype(BF16)
        projected = lax.dot_general(
            normed, wout_ref[...], (((0,), (0,)), ((), ())), preferred_element_type=F32
        )
        for bit in range(2):
            result[pl.ds(bit * 24 + j, 64, stride=49), :] = projected[bit * 64 : bit * 64 + 64]
    for i in range(64):
        rows = slice(i * 48, i * 48 + 48)
        out_ref[rows, :] = (gate_ref[rows, :] * result[i * 49 : i * 49 + 48, :]).astype(BF16)


def shape(dims, kind):
    return jax.ShapeDtypeStruct(dims, kind)


def exchange(values):
    groups = [list(range(core, 2 * LANES, 2)) for core in range(2)]
    return lax.all_to_all(
        values, AXES, split_axis=0, concat_axis=0, axis_index_groups=groups, tiled=True
    )


def shards(z_band, z_square, ln_in_gain, w_a_gate, w_a, w_b_gate, w_b, w_g, ln_out_gain, w_out):
    gain_in = ln_in_gain.reshape(1, LANES)
    gain_out = ln_out_gain.reshape(1, LANES)
    rows = z_band.shape[0] * z_band.shape[1]
    band = z_band.reshape(rows, LANES)
    vmem = pl.BlockSpec(memory_space=pltpu.VMEM)
    hbm = pl.BlockSpec(memory_space=pltpu.HBM)
    edges, band_norm = pl.pallas_call(
        edges_kernel,
        out_shape=(
            pltpu.VMEM((LANES * MESSAGE, LANES), BF16),
            pltpu.VMEM((rows, LANES), BF16),
        ),
        in_specs=[hbm] * 7,
        out_specs=(vmem, vmem),
        scratch_shapes=[
            pltpu.VMEM((rows, LANES), BF16),
            pltpu.VMEM(z_square.shape, BF16),
            pltpu.VMEM((1, LANES), F32),
            pltpu.VMEM((4, LANES, LANES), BF16),
            pltpu.VMEM((rows, LANES), F32),
            pltpu.VMEM((9, 2 * LANES, LANES), BF16),
            pltpu.VMEM((LANES * MESSAGE, LANES), F32),
            pltpu.SemaphoreType.DMA((7,)),
        ],
        compiler_params=params(),
        name="edges",
    )(*[
        pltpu.with_memory_space_constraint(a, pltpu.HBM)
        for a in (band, z_square, gain_in, w_a_gate, w_a, w_b_gate, w_b)
    ])
    core = lax.axis_index("core").astype(jnp.int32).reshape(1)
    edges, core = lax.optimization_barrier((edges, core))
    edges = exchange(edges.reshape(LANES, MESSAGE // 2, 2, LANES)).reshape(edges.shape)
    smem = pl.BlockSpec(memory_space=pltpu.SMEM)
    other, left = pl.pallas_call(
        product_kernel,
        out_shape=(pltpu.VMEM((384, 1024), BF16), pltpu.VMEM((4, 384, 256), BF16)),
        in_specs=[smem, vmem],
        out_specs=(vmem, vmem),
        scratch_shapes=[
            pltpu.VMEM((384, 384), BF16),
            pltpu.VMEM((4, 32 * MESSAGE + 8, LANES), F32),
            pltpu.VMEM((4, 2, 8 * PITCH + 8, LANES), F32),
        ],
        compiler_params=params(),
        name="product",
    )(core, edges)
    other, left, band_norm, gain_out = lax.optimization_barrier((other, left, band_norm, gain_out))
    other = lax.ppermute(other, "core", ((0, 1), (1, 0)))
    own = pl.pallas_call(
        own_kernel,
        out_shape=pltpu.VMEM((384, 1024), F32),
        in_specs=[smem, vmem, vmem],
        out_specs=vmem,
        scratch_shapes=[
            pltpu.VMEM((384, 384), BF16),
            pltpu.VMEM((4, 16 * MESSAGE + 8, LANES), F32),
            pltpu.VMEM((4, 2, 8 * PITCH + 8, LANES), F32),
        ],
        compiler_params=params(),
        name="own",
    )(core, edges, left)
    gate = pl.pallas_call(
        gate_kernel,
        out_shape=shape((rows, LANES), F32),
        compiler_params=params(),
        name="gate",
    )(band_norm, w_g)
    triangle = pl.pallas_call(
        sum_kernel,
        out_shape=pltpu.VMEM((LANES, 24, LANES), BF16),
        compiler_params=params(),
        name="sum",
    )(own, other)
    triangle, gate, gain_out = lax.optimization_barrier((triangle, gate, gain_out))
    triangle = exchange(triangle)
    update = pl.pallas_call(
        update_kernel,
        out_shape=shape((rows, LANES), BF16),
        scratch_shapes=[pltpu.VMEM((LANES * PITCH, LANES), F32), pltpu.VMEM((64 * 49, LANES), F32)],
        compiler_params=params(),
        name="update",
    )(triangle, gate, gain_out, w_out)
    return update.reshape(z_band.shape)


def solution(mesh):
    fine = Mesh(mesh.devices.reshape(tuple(size for _, size in PARTS)), AXES)
    pair = P(("z", "y_lo"), ("x", "y_hi", "core"), None)
    placed = (pair, pair, P(), P(), P(), P(), P(), P(), P(), P())
    return jax.shard_map(
        shards, mesh=fine, in_specs=placed, out_specs=pair, check_vma=False
    )
```

```python
import functools

import jax
import jax.numpy as jnp
from jax import lax
from jax.experimental import pallas as pl
from jax.experimental.pallas import tpu as pltpu
from jax.sharding import Mesh, PartitionSpec as P

F32 = jnp.float32
BF16 = jnp.bfloat16
PARTS = (("z", 8), ("y_lo", 2), ("x", 4), ("y_hi", 2), ("core", 2))
CHIPS = ("z", "y_lo", "x", "y_hi")
ROWS = 16
COLS = 8
LANES = 128
MESSAGE = 42
PITCH = 25
VMEM = 40 * 1024 * 1024


def params():
    return pltpu.CompilerParams(vmem_limit_bytes=VMEM)


def swap(arrays):
    lane = lax.broadcasted_iota(jnp.int32, arrays[0].shape, len(arrays[0].shape) - 1)
    axis = len(arrays[0].shape) - 1
    arrays = list(arrays)
    for bit in range(3):
        shift = 16 << bit
        low = (lane & shift) == 0
        for first in range(8):
            if first & (1 << bit):
                continue
            second = first | (1 << bit)
            a, b = arrays[first], arrays[second]
            if 2 * shift == LANES:
                up = down = pltpu.roll(jnp.where(low, b, a), shift, axis)
            else:
                up, down = pltpu.roll(b, shift, axis), pltpu.roll(a, LANES - shift, axis)
            arrays[first], arrays[second] = jnp.where(low, a, up), jnp.where(low, down, b)
    return arrays


def edges_kernel(
    band_hbm, square_hbm, gain_hbm, wag_hbm, wa_hbm, wbg_hbm, wb_hbm, out_ref, band_norm,
    band, square, gain_ref, weights, normed, square_norm, held, sems,
):
    pairs = [
        (gain_hbm, gain_ref),
        (band_hbm, band),
        (wag_hbm, weights.at[0]),
        (wa_hbm, weights.at[1]),
        (wbg_hbm, weights.at[2]),
        (wb_hbm, weights.at[3]),
        (square_hbm, square),
    ]
    copies = [pltpu.make_async_copy(a, b, sems.at[n]) for n, (a, b) in enumerate(pairs)]
    for copy in copies:
        copy.start()
    share = jnp.full((LANES, LANES), 1.0 / LANES, BF16)
    copies[0].wait()
    gain = gain_ref[...]

    def project(both, rows):
        both = lax.dot_general(both, rows, (((1,), (1,)), ((), ())), preferred_element_type=F32)
        return jax.nn.sigmoid(both[:LANES]) * both[LANES:]

    def normalise(z):
        centred = z.astype(F32) - jnp.dot(z, share, preferred_element_type=F32)
        var = jnp.mean(centred * centred, axis=-1, keepdims=True)
        return centred * lax.rsqrt(var + 1e-05) * gain

    copies[1].wait()
    half = band.shape[0] // 2
    for part in range(2):
        rows = slice(part * half, part * half + half)
        norm = normalise(band[rows, :])
        normed[rows, :] = norm
        band_norm[rows, :] = norm.astype(BF16)
    for copy in copies[2:]:
        copy.wait()
    for step in range(9):
        k3, hi = step // 3, step % 3 * 2
        z = square[hi * 8 : hi * 8 + 16, k3 * 16 : k3 * 16 + 16, :].reshape(2 * LANES, LANES)
        square_norm[step] = normalise(z).astype(BF16)
    left = jnp.concatenate([weights[0].T, weights[1].T], axis=0)
    right = jnp.concatenate([weights[2].T, weights[3].T], axis=0)
    for step in range(12):
        rows = [
            normed[pl.ds(bit * 24 + step * 2 + odd, 64, stride=48), :]
            for odd in range(2)
            for bit in range(2)
        ]
        edge = project(left, jnp.concatenate(rows, axis=0).astype(BF16))
        for odd in range(2):
            kb, kk = divmod(step * 2 + odd, 8)
            held[pl.ds(kk * 3 + kb, LANES, stride=MESSAGE), :] = edge[
                :, odd * LANES : odd * LANES + LANES
            ]
        if step < 9:
            k3, hi = step // 3, step % 3 * 2
            edge = project(right, square_norm[step])
            for odd in range(2):
                held[pl.ds(24 + (hi + odd) * 3 + k3, LANES, stride=MESSAGE), :] = edge[
                    :, odd * LANES : odd * LANES + LANES
                ]
    out_ref[...] = held[...].astype(BF16)


def swap_halves(a, b):
    low = lax.broadcasted_iota(jnp.int32, a.shape, 1) < 64
    moved = pltpu.roll(jnp.where(low, b, a), 64, 1)
    return jnp.where(low, a, moved), jnp.where(low, moved, b)


def arrange_right(rows, right, held, p):
    for k3 in range(3):
        blocks = swap([
            jnp.concatenate([rows(half, q, k3) for half in range(2)], axis=0).astype(BF16)
            for q in range(8)
        ])
        for lo in range(8):
            block = blocks[lo].astype(F32)
            start = lo * PITCH + k3 * 8
            for half in range(2):
                held[half, start : start + 8, :] = block[half * 8 : half * 8 + 8]
    for k3 in range(3):
        for hi in range(6):
            tiles = [held[half, pl.ds(k3 * 8 + hi, 8, stride=PITCH), :] for half in range(2)]
            start = (hi % 2 * 3 + hi // 2) * 64 + p * 16
            right[start : start + 16, k3 * LANES : k3 * LANES + LANES] = jnp.concatenate(tiles, axis=0).astype(BF16)


def multiply(right, left, out_ref):
    for p in range(4):
        out_ref[:, p * 256 : p * 256 + 256] = jnp.dot(
            right[...], left[p], preferred_element_type=F32
        ).astype(out_ref.dtype)


def product_kernel(core_ref, in_ref, other_ref, left, right, raw, held):
    size = 32 * MESSAGE
    there = pl.multiple_of((1 - core_ref[0]) * (8 * MESSAGE), 8)

    for p in range(4):
        raw[p, :size, :] = in_ref[p * size : p * size + size, :].astype(F32)

        def rows(n, kb, p=p):
            return raw[p, pl.ds(n * MESSAGE + kb, 8, stride=3), :]

        def right_rows(half, q, k3, p=p):
            return raw[p, pl.ds(there + ((half * 16 + q) * MESSAGE + 24 + k3), 8, stride=3), :]

        for half in range(2):
            for q in range(8):
                n = half * 16 + q
                pairs = [swap_halves(rows(n, kb), rows(n + 8, kb)) for kb in range(3)]
                blocks = [pair[kbit] for kbit in range(2) for pair in pairs]
                for k3 in range(3):
                    left[
                        p,
                        k3 * LANES + q * 16 : k3 * LANES + q * 16 + 16,
                        half * LANES : half * LANES + LANES,
                    ] = jnp.concatenate(blocks[2 * k3 : 2 * k3 + 2], axis=0).astype(BF16)
        arrange_right(right_rows, right, held.at[p], p)
    multiply(right, left, other_ref)


def own_kernel(core_ref, in_ref, left, own_ref, right, raw, held):
    size = 8 * MESSAGE
    here = core_ref[0] * size

    for p in range(4):
        for half in range(2):
            start = pl.multiple_of((p * 4 + half * 2) * size + here, 16)
            raw[p, half * size : half * size + size, :] = in_ref[pl.ds(start, size), :].astype(F32)

        def right_rows(half, q, k3, p=p):
            return raw[p, pl.ds((half * 8 + q) * MESSAGE + 24 + k3, 8, stride=3), :]

        arrange_right(right_rows, right, held.at[p], p)
    multiply(right, left, own_ref)


def sum_kernel(own_ref, other_ref, out_ref):
    for p in range(8):
        lanes = slice(p * LANES, p * LANES + LANES)
        for q2 in range(4):
            tiles = []
            for jh in range(3):
                a, b = [
                    own_ref[start : start + 16, lanes] + other_ref[start : start + 16, lanes].astype(F32)
                    for start in (jh * 64 + q2 * 16, 192 + jh * 64 + q2 * 16)
                ]
                tiles.append(swap_halves(a, b))
            for odd in range(2):
                for n in range(2):
                    out_ref[(p * 2 + odd) * 8 + q2 * 2 + n] = jnp.concatenate(
                        [tiles[jh][odd][n * 8 : n * 8 + 8] for jh in range(3)], axis=0
                    ).astype(BF16)


def gate_kernel(norm_ref, wg_ref, out_ref):
    out_ref[...] = jax.nn.sigmoid(
        jnp.dot(norm_ref[...], wg_ref[...], preferred_element_type=F32)
    )


def update_kernel(in_ref, gate_ref, gain_ref, wout_ref, out_hbm, held, result, staged, sems):
    for h in range(LANES):
        held[h * PITCH : h * PITCH + 24, :] = in_ref[h].astype(F32)
    gain = jnp.broadcast_to(gain_ref[...], (LANES, LANES)).T
    copies = []
    for jh in range(3):
        for jl in range(8):
            tri = held[pl.ds(jh * 8 + jl, LANES, stride=PITCH), :]
            mean = jnp.mean(tri, axis=0, keepdims=True)
            centred = tri - mean
            var = jnp.mean(centred * centred, axis=0, keepdims=True)
            normed = (centred * lax.rsqrt(var + 1e-05) * gain).astype(BF16)
            projected = lax.dot_general(
                normed, wout_ref[...], (((0,), (0,)), ((), ())), preferred_element_type=F32
            )
            for bit in range(2):
                result[pl.ds(jh * 16 + bit * 8 + jl, 64, stride=49), :] = projected[
                    bit * 64 : bit * 64 + 64
                ]
        block = slice(jh * 16, jh * 16 + 16)
        for i in range(64):
            start = i * 49 + jh * 16
            staged[i, block, :] = (gate_ref[i, block, :] * result[start : start + 16, :]).astype(BF16)
        copies.append(
            pltpu.make_async_copy(staged.at[:, block, :], out_hbm.at[:, block, :], sems.at[jh])
        )
        copies[-1].start()
    for copy in copies:
        copy.wait()


def shape(dims, kind):
    return jax.ShapeDtypeStruct(dims, kind)


def exchange(values):
    return lax.all_to_all(values, CHIPS, split_axis=0, concat_axis=0, tiled=True)


def shards(z_band, z_square, ln_in_gain, w_a_gate, w_a, w_b_gate, w_b, w_g, ln_out_gain, w_out):
    gain_in = ln_in_gain.reshape(1, LANES)
    gain_out = ln_out_gain.reshape(1, LANES)
    rows = z_band.shape[0] * z_band.shape[1]
    band = z_band.reshape(rows, LANES)
    vmem = pl.BlockSpec(memory_space=pltpu.VMEM)
    hbm = pl.BlockSpec(memory_space=pltpu.HBM)
    edges, band_norm = pl.pallas_call(
        edges_kernel,
        out_shape=(
            pltpu.VMEM((LANES * MESSAGE, LANES), BF16),
            pltpu.VMEM((rows, LANES), BF16),
        ),
        in_specs=[hbm] * 7,
        out_specs=(vmem, vmem),
        scratch_shapes=[
            pltpu.VMEM((rows, LANES), BF16),
            pltpu.VMEM(z_square.shape, BF16),
            pltpu.VMEM((1, LANES), F32),
            pltpu.VMEM((4, LANES, LANES), BF16),
            pltpu.VMEM((rows, LANES), F32),
            pltpu.VMEM((9, 2 * LANES, LANES), BF16),
            pltpu.VMEM((LANES * MESSAGE, LANES), F32),
            pltpu.SemaphoreType.DMA((7,)),
        ],
        compiler_params=params(),
        name="edges",
    )(*[
        pltpu.with_memory_space_constraint(a, pltpu.HBM)
        for a in (band, z_square, gain_in, w_a_gate, w_a, w_b_gate, w_b)
    ])
    core = lax.axis_index("core").astype(jnp.int32).reshape(1)
    edges, core = lax.optimization_barrier((edges, core))
    edges = exchange(edges.reshape(LANES, MESSAGE // 2, 2, LANES)).reshape(edges.shape)
    smem = pl.BlockSpec(memory_space=pltpu.SMEM)
    other, left = pl.pallas_call(
        product_kernel,
        out_shape=(pltpu.VMEM((384, 1024), BF16), pltpu.VMEM((4, 384, 256), BF16)),
        in_specs=[smem, vmem],
        out_specs=(vmem, vmem),
        scratch_shapes=[
            pltpu.VMEM((384, 384), BF16),
            pltpu.VMEM((4, 32 * MESSAGE + 8, LANES), F32),
            pltpu.VMEM((4, 2, 8 * PITCH + 8, LANES), F32),
        ],
        compiler_params=params(),
        name="product",
    )(core, edges)
    other, left, band_norm, gain_out = lax.optimization_barrier((other, left, band_norm, gain_out))
    other = lax.ppermute(other, "core", ((0, 1), (1, 0)))
    own = pl.pallas_call(
        own_kernel,
        out_shape=pltpu.VMEM((384, 1024), F32),
        in_specs=[smem, vmem, vmem],
        out_specs=vmem,
        scratch_shapes=[
            pltpu.VMEM((384, 384), BF16),
            pltpu.VMEM((4, 16 * MESSAGE + 8, LANES), F32),
            pltpu.VMEM((4, 2, 8 * PITCH + 8, LANES), F32),
        ],
        compiler_params=params(),
        name="own",
    )(core, edges, left)
    gate = pl.pallas_call(
        gate_kernel,
        out_shape=shape((rows, LANES), F32),
        compiler_params=params(),
        name="gate",
    )(band_norm, w_g)
    triangle = pl.pallas_call(
        sum_kernel,
        out_shape=pltpu.VMEM((LANES, 24, LANES), BF16),
        compiler_params=params(),
        name="sum",
    )(own, other)
    triangle, gate, gain_out = lax.optimization_barrier((triangle, gate, gain_out))
    triangle = exchange(triangle)
    return pl.pallas_call(
        update_kernel,
        out_shape=shape(z_band.shape, BF16),
        out_specs=hbm,
        scratch_shapes=[
            pltpu.VMEM((LANES * PITCH, LANES), F32),
            pltpu.VMEM((64 * 49, LANES), F32),
            pltpu.VMEM(z_band.shape, BF16),
            pltpu.SemaphoreType.DMA((3,)),
        ],
        compiler_params=params(),
        name="update",
    )(triangle, gate.reshape(z_band.shape), gain_out, w_out)


def solution(mesh):
    names = tuple(name for name, _ in PARTS)
    fine = Mesh(mesh.devices.reshape(tuple(size for _, size in PARTS)), names)
    pair = P(("z", "y_lo"), ("x", "y_hi", "core"), None)
    placed = (pair, pair, P(), P(), P(), P(), P(), P(), P(), P())
    return jax.shard_map(
        shards, mesh=fine, in_specs=placed, out_specs=pair, check_vma=False
    )
```

```python
import functools

import jax
import jax.numpy as jnp
from jax import lax
from jax.experimental import pallas as pl
from jax.experimental.pallas import tpu as pltpu
from jax.sharding import Mesh, PartitionSpec as P

F32 = jnp.float32
BF16 = jnp.bfloat16
PARTS = (("z", 8), ("y_lo", 2), ("x", 4), ("y_hi", 2), ("core", 2))
CHIPS = ("z", "y_lo", "x", "y_hi")
ROWS = 16
COLS = 8
LANES = 128
MESSAGE = 42
PITCH = 25
VMEM = 40 * 1024 * 1024


def params():
    return pltpu.CompilerParams(vmem_limit_bytes=VMEM)


def swap(arrays):
    lane = lax.broadcasted_iota(jnp.int32, arrays[0].shape, len(arrays[0].shape) - 1)
    axis = len(arrays[0].shape) - 1
    arrays = list(arrays)
    for bit in range(3):
        shift = 16 << bit
        low = (lane & shift) == 0
        for first in range(8):
            if first & (1 << bit):
                continue
            second = first | (1 << bit)
            a, b = arrays[first], arrays[second]
            if 2 * shift == LANES:
                up = down = pltpu.roll(jnp.where(low, b, a), shift, axis)
            else:
                up, down = pltpu.roll(b, shift, axis), pltpu.roll(a, LANES - shift, axis)
            arrays[first], arrays[second] = jnp.where(low, a, up), jnp.where(low, down, b)
    return arrays


def edges_kernel(
    band_hbm, square_hbm, gain_hbm, wag_hbm, wa_hbm, wbg_hbm, wb_hbm, out_ref, band_norm,
    band, square, gain_ref, weights, normed, square_norm, held, sems,
):
    pairs = [
        (gain_hbm, gain_ref),
        (band_hbm, band),
        (wag_hbm, weights.at[0]),
        (wa_hbm, weights.at[1]),
        (wbg_hbm, weights.at[2]),
        (wb_hbm, weights.at[3]),
        (square_hbm, square),
    ]
    copies = [pltpu.make_async_copy(a, b, sems.at[n]) for n, (a, b) in enumerate(pairs)]
    for copy in copies:
        copy.start()
    share = jnp.full((LANES, LANES), 1.0 / LANES, BF16)
    copies[0].wait()
    gain = gain_ref[...]

    def project(both, rows):
        both = lax.dot_general(both, rows, (((1,), (1,)), ((), ())), preferred_element_type=F32)
        return jax.nn.sigmoid(both[:LANES]) * both[LANES:]

    def normalise(z):
        centred = z.astype(F32) - jnp.dot(z, share, preferred_element_type=F32)
        var = jnp.mean(centred * centred, axis=-1, keepdims=True)
        return centred * lax.rsqrt(var + 1e-05) * gain

    copies[1].wait()
    half = band.shape[0] // 2
    for part in range(2):
        rows = slice(part * half, part * half + half)
        norm = normalise(band[rows, :])
        normed[rows, :] = norm
        band_norm[rows, :] = norm.astype(BF16)
    for copy in copies[2:]:
        copy.wait()
    for step in range(9):
        k3, hi = step // 3, step % 3 * 2
        z = square[hi * 8 : hi * 8 + 16, k3 * 16 : k3 * 16 + 16, :].reshape(2 * LANES, LANES)
        square_norm[step] = normalise(z).astype(BF16)
    left = jnp.concatenate([weights[0].T, weights[1].T], axis=0)
    right = jnp.concatenate([weights[2].T, weights[3].T], axis=0)
    for step in range(12):
        rows = [
            normed[pl.ds(bit * 24 + step * 2 + odd, 64, stride=48), :]
            for odd in range(2)
            for bit in range(2)
        ]
        edge = project(left, jnp.concatenate(rows, axis=0).astype(BF16))
        for odd in range(2):
            kb, kk = divmod(step * 2 + odd, 8)
            held[pl.ds(kk * 3 + kb, LANES, stride=MESSAGE), :] = edge[
                :, odd * LANES : odd * LANES + LANES
            ]
        if step < 9:
            k3, hi = step // 3, step % 3 * 2
            edge = project(right, square_norm[step])
            for odd in range(2):
                held[pl.ds(24 + (hi + odd) * 3 + k3, LANES, stride=MESSAGE), :] = edge[
                    :, odd * LANES : odd * LANES + LANES
                ]
    out_ref[...] = held[...].astype(BF16)


def swap_halves(a, b):
    low = lax.broadcasted_iota(jnp.int32, a.shape, 1) < 64
    moved = pltpu.roll(jnp.where(low, b, a), 64, 1)
    return jnp.where(low, a, moved), jnp.where(low, moved, b)


def arrange_right(rows, right, held, p):
    for k3 in range(3):
        blocks = swap([
            jnp.concatenate([rows(half, q, k3) for half in range(2)], axis=0).astype(BF16)
            for q in range(8)
        ])
        for lo in range(8):
            block = blocks[lo].astype(F32)
            start = lo * PITCH + k3 * 8
            for half in range(2):
                held[half, start : start + 8, :] = block[half * 8 : half * 8 + 8]
    for k3 in range(3):
        for hi in range(6):
            tiles = [held[half, pl.ds(k3 * 8 + hi, 8, stride=PITCH), :] for half in range(2)]
            start = (hi % 2 * 3 + hi // 2) * 64 + p * 16
            right[start : start + 16, k3 * LANES : k3 * LANES + LANES] = jnp.concatenate(tiles, axis=0).astype(BF16)


def multiply(right, left, out_ref, parts=range(4)):
    for n, p in enumerate(parts):
        out_ref[:, n * 256 : n * 256 + 256] = jnp.dot(
            right[...], left[p], preferred_element_type=F32
        ).astype(out_ref.dtype)


def product_kernel(core_ref, in_ref, first_ref, second_ref, left, right, raw, held):
    size = 32 * MESSAGE
    there = pl.multiple_of((1 - core_ref[0]) * (8 * MESSAGE), 8)

    for p in range(4):
        raw[p, :size, :] = in_ref[p * size : p * size + size, :].astype(F32)

        def rows(n, kb, p=p):
            return raw[p, pl.ds(n * MESSAGE + kb, 8, stride=3), :]

        def right_rows(half, q, k3, p=p):
            return raw[p, pl.ds(there + ((half * 16 + q) * MESSAGE + 24 + k3), 8, stride=3), :]

        for half in range(2):
            for q in range(8):
                n = half * 16 + q
                pairs = [swap_halves(rows(n, kb), rows(n + 8, kb)) for kb in range(3)]
                blocks = [pair[kbit] for kbit in range(2) for pair in pairs]
                for k3 in range(3):
                    left[
                        p,
                        k3 * LANES + q * 16 : k3 * LANES + q * 16 + 16,
                        half * LANES : half * LANES + LANES,
                    ] = jnp.concatenate(blocks[2 * k3 : 2 * k3 + 2], axis=0).astype(BF16)
        arrange_right(right_rows, right, held.at[p], p)
    multiply(right, left, first_ref, (0, 1))
    multiply(right, left, second_ref, (2, 3))


def own_kernel(core_ref, in_ref, left, own_ref, right, raw, held):
    size = 8 * MESSAGE
    here = core_ref[0] * size

    for p in range(4):
        for half in range(2):
            start = pl.multiple_of((p * 4 + half * 2) * size + here, 16)
            raw[p, half * size : half * size + size, :] = in_ref[pl.ds(start, size), :].astype(F32)

        def right_rows(half, q, k3, p=p):
            return raw[p, pl.ds((half * 8 + q) * MESSAGE + 24 + k3, 8, stride=3), :]

        arrange_right(right_rows, right, held.at[p], p)
    multiply(right, left, own_ref)


def sum_kernel(own_ref, first_ref, second_ref, out_ref):
    for p in range(8):
        other_ref = (first_ref, second_ref)[p // 4]
        lanes = slice(p * LANES, p * LANES + LANES)
        there = slice(p % 4 * LANES, p % 4 * LANES + LANES)
        for q2 in range(4):
            tiles = []
            for jh in range(3):
                a, b = [
                    own_ref[start : start + 16, lanes] + other_ref[start : start + 16, there].astype(F32)
                    for start in (jh * 64 + q2 * 16, 192 + jh * 64 + q2 * 16)
                ]
                tiles.append(swap_halves(a, b))
            for odd in range(2):
                for n in range(2):
                    out_ref[(p * 2 + odd) * 8 + q2 * 2 + n] = jnp.concatenate(
                        [tiles[jh][odd][n * 8 : n * 8 + 8] for jh in range(3)], axis=0
                    ).astype(BF16)


def gate_kernel(norm_ref, wg_ref, out_ref):
    out_ref[...] = jax.nn.sigmoid(
        jnp.dot(norm_ref[...], wg_ref[...], preferred_element_type=F32)
    )


def update_kernel(in_ref, gate_ref, gain_ref, wout_ref, out_hbm, held, result, staged, sems):
    for h in range(LANES):
        held[h * PITCH : h * PITCH + 24, :] = in_ref[h].astype(F32)
    gain = jnp.broadcast_to(gain_ref[...], (LANES, LANES)).T
    copies = []
    for jh in range(3):
        for jl in range(8):
            tri = held[pl.ds(jh * 8 + jl, LANES, stride=PITCH), :]
            mean = jnp.mean(tri, axis=0, keepdims=True)
            centred = tri - mean
            var = jnp.mean(centred * centred, axis=0, keepdims=True)
            normed = (centred * lax.rsqrt(var + 1e-05) * gain).astype(BF16)
            projected = lax.dot_general(
                normed, wout_ref[...], (((0,), (0,)), ((), ())), preferred_element_type=F32
            )
            for bit in range(2):
                result[pl.ds(jh * 16 + bit * 8 + jl, 64, stride=49), :] = projected[
                    bit * 64 : bit * 64 + 64
                ]
        block = slice(jh * 16, jh * 16 + 16)
        for i in range(64):
            start = i * 49 + jh * 16
            staged[i, block, :] = (gate_ref[i, block, :] * result[start : start + 16, :]).astype(BF16)
        copies.append(
            pltpu.make_async_copy(staged.at[:, block, :], out_hbm.at[:, block, :], sems.at[jh])
        )
        copies[-1].start()
    for copy in copies:
        copy.wait()


def shape(dims, kind):
    return jax.ShapeDtypeStruct(dims, kind)


def exchange(values):
    return lax.all_to_all(values, CHIPS, split_axis=0, concat_axis=0, tiled=True)


def shards(z_band, z_square, ln_in_gain, w_a_gate, w_a, w_b_gate, w_b, w_g, ln_out_gain, w_out):
    gain_in = ln_in_gain.reshape(1, LANES)
    gain_out = ln_out_gain.reshape(1, LANES)
    rows = z_band.shape[0] * z_band.shape[1]
    band = z_band.reshape(rows, LANES)
    vmem = pl.BlockSpec(memory_space=pltpu.VMEM)
    hbm = pl.BlockSpec(memory_space=pltpu.HBM)
    edges, band_norm = pl.pallas_call(
        edges_kernel,
        out_shape=(
            pltpu.VMEM((LANES * MESSAGE, LANES), BF16),
            pltpu.VMEM((rows, LANES), BF16),
        ),
        in_specs=[hbm] * 7,
        out_specs=(vmem, vmem),
        scratch_shapes=[
            pltpu.VMEM((rows, LANES), BF16),
            pltpu.VMEM(z_square.shape, BF16),
            pltpu.VMEM((1, LANES), F32),
            pltpu.VMEM((4, LANES, LANES), BF16),
            pltpu.VMEM((rows, LANES), F32),
            pltpu.VMEM((9, 2 * LANES, LANES), BF16),
            pltpu.VMEM((LANES * MESSAGE, LANES), F32),
            pltpu.SemaphoreType.DMA((7,)),
        ],
        compiler_params=params(),
        name="edges",
    )(*[
        pltpu.with_memory_space_constraint(a, pltpu.HBM)
        for a in (band, z_square, gain_in, w_a_gate, w_a, w_b_gate, w_b)
    ])
    core = lax.axis_index("core").astype(jnp.int32).reshape(1)
    edges, core = lax.optimization_barrier((edges, core))
    edges = exchange(edges.reshape(LANES, MESSAGE // 2, 2, LANES)).reshape(edges.shape)
    smem = pl.BlockSpec(memory_space=pltpu.SMEM)
    first, second, left = pl.pallas_call(
        product_kernel,
        out_shape=(
            pltpu.VMEM((384, 512), BF16),
            pltpu.VMEM((384, 512), BF16),
            pltpu.VMEM((4, 384, 256), BF16),
        ),
        in_specs=[smem, vmem],
        out_specs=(vmem, vmem, vmem),
        scratch_shapes=[
            pltpu.VMEM((384, 384), BF16),
            pltpu.VMEM((4, 32 * MESSAGE + 8, LANES), F32),
            pltpu.VMEM((4, 2, 8 * PITCH + 8, LANES), F32),
        ],
        compiler_params=params(),
        name="product",
    )(core, edges)
    first, second, left, band_norm, gain_out = lax.optimization_barrier(
        (first, second, left, band_norm, gain_out)
    )
    first = lax.ppermute(first, "core", ((0, 1), (1, 0)))
    second = lax.ppermute(second, "core", ((0, 1), (1, 0)))
    own = pl.pallas_call(
        own_kernel,
        out_shape=pltpu.VMEM((384, 1024), F32),
        in_specs=[smem, vmem, vmem],
        out_specs=vmem,
        scratch_shapes=[
            pltpu.VMEM((384, 384), BF16),
            pltpu.VMEM((4, 16 * MESSAGE + 8, LANES), F32),
            pltpu.VMEM((4, 2, 8 * PITCH + 8, LANES), F32),
        ],
        compiler_params=params(),
        name="own",
    )(core, edges, left)
    gate = pl.pallas_call(
        gate_kernel,
        out_shape=shape((rows, LANES), F32),
        compiler_params=params(),
        name="gate",
    )(band_norm, w_g)
    triangle = pl.pallas_call(
        sum_kernel,
        out_shape=pltpu.VMEM((LANES, 24, LANES), BF16),
        compiler_params=params(),
        name="sum",
    )(own, first, second)
    triangle, gate, gain_out = lax.optimization_barrier((triangle, gate, gain_out))
    triangle = exchange(triangle)
    return pl.pallas_call(
        update_kernel,
        out_shape=shape(z_band.shape, BF16),
        out_specs=hbm,
        scratch_shapes=[
            pltpu.VMEM((LANES * PITCH, LANES), F32),
            pltpu.VMEM((64 * 49, LANES), F32),
            pltpu.VMEM(z_band.shape, BF16),
            pltpu.SemaphoreType.DMA((3,)),
        ],
        compiler_params=params(),
        name="update",
    )(triangle, gate.reshape(z_band.shape), gain_out, w_out)


def solution(mesh):
    names = tuple(name for name, _ in PARTS)
    fine = Mesh(mesh.devices.reshape(tuple(size for _, size in PARTS)), names)
    pair = P(("z", "y_lo"), ("x", "y_hi", "core"), None)
    placed = (pair, pair, P(), P(), P(), P(), P(), P(), P(), P())
    return jax.shard_map(
        shards, mesh=fine, in_specs=placed, out_specs=pair, check_vma=False
    )
```

```python
import functools

import jax
import jax.numpy as jnp
from jax import lax
from jax.experimental import pallas as pl
from jax.experimental.pallas import tpu as pltpu
from jax.sharding import Mesh, PartitionSpec as P

F32 = jnp.float32
BF16 = jnp.bfloat16
PARTS = (("z", 8), ("y_lo", 2), ("x", 4), ("y_hi", 2), ("core", 2))
CHIPS = ("z", "y_lo", "x", "y_hi")
ROWS = 16
COLS = 8
LANES = 128
MESSAGE = 42
PITCH = 25
VMEM = 40 * 1024 * 1024


def params():
    return pltpu.CompilerParams(vmem_limit_bytes=VMEM)


def swap(arrays):
    lane = lax.broadcasted_iota(jnp.int32, arrays[0].shape, len(arrays[0].shape) - 1)
    axis = len(arrays[0].shape) - 1
    arrays = list(arrays)
    for bit in range(3):
        shift = 16 << bit
        low = (lane & shift) == 0
        for first in range(8):
            if first & (1 << bit):
                continue
            second = first | (1 << bit)
            a, b = arrays[first], arrays[second]
            if 2 * shift == LANES:
                up = down = pltpu.roll(jnp.where(low, b, a), shift, axis)
            else:
                up, down = pltpu.roll(b, shift, axis), pltpu.roll(a, LANES - shift, axis)
            arrays[first], arrays[second] = jnp.where(low, a, up), jnp.where(low, down, b)
    return arrays


def edges_kernel(
    band_hbm, square_hbm, gain_hbm, wag_hbm, wa_hbm, wbg_hbm, wb_hbm, out_ref, band_norm,
    band, square, gain_ref, weights, normed, square_norm, held, sems,
):
    pairs = [
        (gain_hbm, gain_ref),
        (band_hbm, band),
        (wag_hbm, weights.at[0]),
        (wa_hbm, weights.at[1]),
        (wbg_hbm, weights.at[2]),
        (wb_hbm, weights.at[3]),
        (square_hbm, square),
    ]
    copies = [pltpu.make_async_copy(a, b, sems.at[n]) for n, (a, b) in enumerate(pairs)]
    for copy in copies:
        copy.start()
    share = jnp.full((LANES, LANES), 1.0 / LANES, BF16)
    copies[0].wait()
    gain = gain_ref[...]

    def project(both, rows):
        both = lax.dot_general(both, rows, (((1,), (1,)), ((), ())), preferred_element_type=F32)
        return jax.nn.sigmoid(both[:LANES]) * both[LANES:]

    def normalise(z):
        centred = z.astype(F32) - jnp.dot(z, share, preferred_element_type=F32)
        var = jnp.mean(centred * centred, axis=-1, keepdims=True)
        return centred * lax.rsqrt(var + 1e-05) * gain

    copies[1].wait()
    half = band.shape[0] // 2
    for part in range(2):
        rows = slice(part * half, part * half + half)
        norm = normalise(band[rows, :])
        normed[rows, :] = norm
        band_norm[rows, :] = norm.astype(BF16)
    for copy in copies[2:]:
        copy.wait()
    for step in range(9):
        k3, hi = step // 3, step % 3 * 2
        z = square[hi * 8 : hi * 8 + 16, k3 * 16 : k3 * 16 + 16, :].reshape(2 * LANES, LANES)
        square_norm[step] = normalise(z).astype(BF16)
    left = jnp.concatenate([weights[0].T, weights[1].T], axis=0)
    right = jnp.concatenate([weights[2].T, weights[3].T], axis=0)
    for step in range(12):
        rows = [
            normed[pl.ds(bit * 24 + step * 2 + odd, 64, stride=48), :]
            for odd in range(2)
            for bit in range(2)
        ]
        edge = project(left, jnp.concatenate(rows, axis=0).astype(BF16))
        for odd in range(2):
            kb, kk = divmod(step * 2 + odd, 8)
            held[pl.ds(kk * 3 + kb, LANES, stride=MESSAGE), :] = edge[
                :, odd * LANES : odd * LANES + LANES
            ]
        if step < 9:
            k3, hi = step // 3, step % 3 * 2
            edge = project(right, square_norm[step])
            for odd in range(2):
                held[pl.ds(24 + (hi + odd) * 3 + k3, LANES, stride=MESSAGE), :] = edge[
                    :, odd * LANES : odd * LANES + LANES
                ]
    out_ref[...] = held[...].astype(BF16)


def swap_halves(a, b):
    low = lax.broadcasted_iota(jnp.int32, a.shape, 1) < 64
    moved = pltpu.roll(jnp.where(low, b, a), 64, 1)
    return jnp.where(low, a, moved), jnp.where(low, moved, b)


def arrange_right(rows, right, held, p):
    for k3 in range(3):
        blocks = swap([
            jnp.concatenate([rows(half, q, k3) for half in range(2)], axis=0).astype(BF16)
            for q in range(8)
        ])
        for lo in range(8):
            block = blocks[lo].astype(F32)
            start = lo * PITCH + k3 * 8
            for half in range(2):
                held[half, start : start + 8, :] = block[half * 8 : half * 8 + 8]
    for k3 in range(3):
        for hi in range(6):
            tiles = [held[half, pl.ds(k3 * 8 + hi, 8, stride=PITCH), :] for half in range(2)]
            start = (hi % 2 * 3 + hi // 2) * 64 + p * 16
            right[start : start + 16, k3 * LANES : k3 * LANES + LANES] = jnp.concatenate(tiles, axis=0).astype(BF16)


def multiply(right, left, out_ref):
    for p in range(4):
        out_ref[:, p * 256 : p * 256 + 256] = jnp.dot(
            right[...], left[p], preferred_element_type=F32
        ).astype(out_ref.dtype)


def product_kernel(core_ref, in_ref, other_ref, left, right, raw, held):
    size = 32 * MESSAGE
    there = pl.multiple_of((1 - core_ref[0]) * (8 * MESSAGE), 8)

    for p in range(4):
        raw[p, :size, :] = in_ref[p * size : p * size + size, :].astype(F32)

        def rows(n, kb, p=p):
            return raw[p, pl.ds(n * MESSAGE + kb, 8, stride=3), :]

        def right_rows(half, q, k3, p=p):
            return raw[p, pl.ds(there + ((half * 16 + q) * MESSAGE + 24 + k3), 8, stride=3), :]

        for half in range(2):
            for q in range(8):
                n = half * 16 + q
                pairs = [swap_halves(rows(n, kb), rows(n + 8, kb)) for kb in range(3)]
                blocks = [pair[kbit] for kbit in range(2) for pair in pairs]
                for k3 in range(3):
                    left[
                        p,
                        k3 * LANES + q * 16 : k3 * LANES + q * 16 + 16,
                        half * LANES : half * LANES + LANES,
                    ] = jnp.concatenate(blocks[2 * k3 : 2 * k3 + 2], axis=0).astype(BF16)
        arrange_right(right_rows, right, held.at[p], p)
    multiply(right, left, other_ref)


def own_kernel(core_ref, in_ref, left, own_ref, right, raw, held):
    size = 8 * MESSAGE
    here = core_ref[0] * size

    for p in range(4):
        for half in range(2):
            start = pl.multiple_of((p * 4 + half * 2) * size + here, 16)
            raw[p, half * size : half * size + size, :] = in_ref[pl.ds(start, size), :].astype(F32)

        def right_rows(half, q, k3, p=p):
            return raw[p, pl.ds((half * 8 + q) * MESSAGE + 24 + k3, 8, stride=3), :]

        arrange_right(right_rows, right, held.at[p], p)
    multiply(right, left, own_ref)


def sum_kernel(own_ref, other_ref, out_ref):
    for p in range(8):
        lanes = slice(p * LANES, p * LANES + LANES)
        for q2 in range(4):
            tiles = []
            for jh in range(3):
                a, b = [
                    own_ref[start : start + 16, lanes] + other_ref[start : start + 16, lanes].astype(F32)
                    for start in (jh * 64 + q2 * 16, 192 + jh * 64 + q2 * 16)
                ]
                tiles.append(swap_halves(a, b))
            for odd in range(2):
                for n in range(2):
                    out_ref[(p * 2 + odd) * 8 + q2 * 2 + n] = jnp.concatenate(
                        [tiles[jh][odd][n * 8 : n * 8 + 8] for jh in range(3)], axis=0
                    ).astype(BF16)


def gate_kernel(norm_ref, wg_ref, out_ref):
    out_ref[...] = jax.nn.sigmoid(
        jnp.dot(norm_ref[...], wg_ref[...], preferred_element_type=F32)
    )


def update_kernel(in_ref, gate_ref, gain_ref, wout_ref, out_hbm, held, result, staged, sems):
    for h in range(LANES):
        held[h * PITCH : h * PITCH + 24, :] = in_ref[h].astype(F32)
    gain = jnp.broadcast_to(gain_ref[...], (LANES, LANES)).T
    copies = []
    for jh in range(3):
        for jl in range(8):
            tri = held[pl.ds(jh * 8 + jl, LANES, stride=PITCH), :]
            mean = jnp.mean(tri, axis=0, keepdims=True)
            centred = tri - mean
            var = jnp.mean(centred * centred, axis=0, keepdims=True)
            normed = (centred * lax.rsqrt(var + 1e-05) * gain).astype(BF16)
            projected = lax.dot_general(
                normed, wout_ref[...], (((0,), (0,)), ((), ())), preferred_element_type=F32
            )
            for bit in range(2):
                result[pl.ds(jh * 16 + bit * 8 + jl, 64, stride=49), :] = projected[
                    bit * 64 : bit * 64 + 64
                ]
        block = slice(jh * 16, jh * 16 + 16)
        for i in range(64):
            start = i * 49 + jh * 16
            staged[i, block, :] = (gate_ref[i, block, :] * result[start : start + 16, :]).astype(BF16)
        copies.append(
            pltpu.make_async_copy(staged.at[:, block, :], out_hbm.at[:, block, :], sems.at[jh])
        )
        copies[-1].start()
    for copy in copies:
        copy.wait()


def shape(dims, kind):
    return jax.ShapeDtypeStruct(dims, kind)


def exchange(values):
    return lax.all_to_all(values, CHIPS, split_axis=0, concat_axis=0, tiled=True)


def shards(z_band, z_square, ln_in_gain, w_a_gate, w_a, w_b_gate, w_b, w_g, ln_out_gain, w_out):
    gain_in = ln_in_gain.reshape(1, LANES)
    gain_out = ln_out_gain.reshape(1, LANES)
    rows = z_band.shape[0] * z_band.shape[1]
    band = z_band.reshape(rows, LANES)
    vmem = pl.BlockSpec(memory_space=pltpu.VMEM)
    hbm = pl.BlockSpec(memory_space=pltpu.HBM)
    edges, band_norm = pl.pallas_call(
        edges_kernel,
        out_shape=(
            pltpu.VMEM((LANES * MESSAGE, LANES), BF16),
            pltpu.VMEM((rows, LANES), BF16),
        ),
        in_specs=[hbm] * 7,
        out_specs=(vmem, vmem),
        scratch_shapes=[
            pltpu.VMEM((rows, LANES), BF16),
            pltpu.VMEM(z_square.shape, BF16),
            pltpu.VMEM((1, LANES), F32),
            pltpu.VMEM((4, LANES, LANES), BF16),
            pltpu.VMEM((rows, LANES), F32),
            pltpu.VMEM((9, 2 * LANES, LANES), BF16),
            pltpu.VMEM((LANES * MESSAGE, LANES), F32),
            pltpu.SemaphoreType.DMA((7,)),
        ],
        compiler_params=params(),
        name="edges",
    )(*[
        pltpu.with_memory_space_constraint(a, pltpu.HBM)
        for a in (band, z_square, gain_in, w_a_gate, w_a, w_b_gate, w_b)
    ])
    core = lax.axis_index("core").astype(jnp.int32).reshape(1)
    edges, core = lax.optimization_barrier((edges, core))
    edges = exchange(edges.reshape(LANES, MESSAGE // 2, 2, LANES)).reshape(edges.shape)
    smem = pl.BlockSpec(memory_space=pltpu.SMEM)
    other, left = pl.pallas_call(
        product_kernel,
        out_shape=(pltpu.VMEM((384, 1024), BF16), pltpu.VMEM((4, 384, 256), BF16)),
        in_specs=[smem, vmem],
        out_specs=(vmem, vmem),
        scratch_shapes=[
            pltpu.VMEM((384, 384), BF16),
            pltpu.VMEM((4, 32 * MESSAGE + 8, LANES), F32),
            pltpu.VMEM((4, 2, 8 * PITCH + 8, LANES), F32),
        ],
        compiler_params=params(),
        name="product",
    )(core, edges)
    other, left, band_norm, gain_out = lax.optimization_barrier((other, left, band_norm, gain_out))
    other = lax.ppermute(other, "core", ((0, 1), (1, 0)))
    own = pl.pallas_call(
        own_kernel,
        out_shape=pltpu.VMEM((384, 1024), F32),
        in_specs=[smem, vmem, vmem],
        out_specs=vmem,
        scratch_shapes=[
            pltpu.VMEM((384, 384), BF16),
            pltpu.VMEM((4, 16 * MESSAGE + 8, LANES), F32),
            pltpu.VMEM((4, 2, 8 * PITCH + 8, LANES), F32),
        ],
        compiler_params=params(),
        name="own",
    )(core, edges, left)
    gate = pl.pallas_call(
        gate_kernel,
        out_shape=shape((rows, LANES), F32),
        compiler_params=params(),
        name="gate",
    )(band_norm, w_g)
    triangle = pl.pallas_call(
        sum_kernel,
        out_shape=pltpu.VMEM((LANES, 24, LANES), BF16),
        compiler_params=params(),
        name="sum",
    )(own, other)
    triangle, gate, gain_out = lax.optimization_barrier((triangle, gate, gain_out))
    triangle = exchange(triangle.reshape(LANES, 12, 2, LANES)).reshape(triangle.shape)
    return pl.pallas_call(
        update_kernel,
        out_shape=shape(z_band.shape, BF16),
        out_specs=hbm,
        scratch_shapes=[
            pltpu.VMEM((LANES * PITCH, LANES), F32),
            pltpu.VMEM((64 * 49, LANES), F32),
            pltpu.VMEM(z_band.shape, BF16),
            pltpu.SemaphoreType.DMA((3,)),
        ],
        compiler_params=params(),
        name="update",
    )(triangle, gate.reshape(z_band.shape), gain_out, w_out)


def solution(mesh):
    names = tuple(name for name, _ in PARTS)
    fine = Mesh(mesh.devices.reshape(tuple(size for _, size in PARTS)), names)
    pair = P(("z", "y_lo"), ("x", "y_hi", "core"), None)
    placed = (pair, pair, P(), P(), P(), P(), P(), P(), P(), P())
    return jax.shard_map(
        shards, mesh=fine, in_specs=placed, out_specs=pair, check_vma=False
    )
```
